32 devices in a mesh: opg: 8 (over z, x), sec: 4 (over y, core).
Axes of the slice: x: 2, y: 2, z: 4, core: 2. Of those that a mesh axis runs over, the one named last changes fastest.
Arguments:
- psi: bfloat16 [8, 384, 384], P('sec'), may hold values from -6 to 6
- left_ops: bfloat16 [64, 8, 384, 384], P('opg', 'sec'), may hold values from -0.15625 to 0.15625
- right_ops: bfloat16 [64, 8, 384, 384], P('opg', 'sec'), may hold values from -0.109375 to 0.109375
- source: int32 [64, 8], P('opg', 'sec'), may hold values from 0 to 7
- coef_index: int32 [64, 8], P('opg', 'sec'), may hold values from 0 to 63
- sixj: float32 [64], replicated, may hold values from -1 to 1
Outputs:
- sigma: bfloat16 [384, 8, 384], P('opg', 'sec')
The draws below stay inside these ranges and needn't reach their ends.
All inputs are finite; a program needn't handle non-finite values.
Results may differ from the reference program's by a relative error of at most 0.005.
Values may be sent and summed in bfloat16 or wider, within the bound.
No kernel may reach another device: no remote copies, remote signals or barrier semaphores. Data moves between devices by JAX's collectives and lax.ppermute only.
A program may use at most 64 MiB of HBM per device.

```python
import jax
import jax.numpy as jnp
from jax import lax

SB = 384
P_DEV = 8
NJ = 64
NS = 8
PAIRS = 64


def with_ends(drawn, rng, smallest, largest):
    longest = drawn.shape.index(max(drawn.shape))
    spots = []
    for shift in (0, 1):
        where = [jax.random.randint(jax.random.fold_in(rng, axis), (), 0, length) for axis, length in enumerate(drawn.shape)]
        where[longest] = (where[longest] + shift) % drawn.shape[longest]
        spots.append(tuple(where))
    return drawn.at[spots[0]].set(smallest).at[spots[1]].set(largest)


def levels(rng, extent, shards, smallest, largest):
    def one(position, parts):
        draws = jax.random.uniform(jax.random.fold_in(jax.random.fold_in(rng, 6), position), (parts,), jnp.float32, smallest / len(shards), largest / len(shards))
        return jnp.repeat(jnp.exp(draws), extent[position] // parts).reshape((-1,) + (1,) * (len(extent) - position - 1))

    gain = one(*shards[0])
    for cut in shards[1:]:
        gain = gain * one(*cut)
    return gain


def normal_values(own_key, shape, deviation, limit, shards=(), dtype=jnp.bfloat16):
    loudness = levels(own_key, shape, shards, -0.22, 0.18) if shards else 1.0
    values = jax.random.normal(own_key, shape, jnp.float32) * deviation * loudness
    return jnp.minimum(jnp.maximum(values, -limit), limit).astype(dtype)


def setup_inputs(seed: int = 0) -> dict:
    streams_of = jax.random.split(jax.random.key(seed), 7)
    psi = normal_values(streams_of[0], (NS, SB, SB), 1.0, 6.0, ((0, 4),))
    left_ops = normal_values(streams_of[1], (PAIRS, NS, SB, SB), (SB * 4) ** -0.5, 0.15625, ((0, 8), (1, 4)))
    right_ops = normal_values(streams_of[2], (PAIRS, NS, SB, SB), (SB * P_DEV) ** -0.5, 0.109375, ((0, 8), (1, 4)))
    source = with_ends(jax.random.randint(streams_of[3], (PAIRS, NS), 0, NS), jax.random.fold_in(streams_of[3], 1), 0, NS - 1).astype(jnp.int32)
    coef_index = with_ends(jax.random.randint(streams_of[4], (PAIRS, NS), 0, NJ), jax.random.fold_in(streams_of[4], 1), 0, NJ - 1).astype(jnp.int32)
    sixj = jnp.clip(jax.random.uniform(streams_of[5], (NJ,), jnp.float32, -1.0, 1.0), -1.0, 1.0)
    return {"psi": psi, "left_ops": left_ops, "right_ops": right_ops, "source": source, "coef_index": coef_index, "sixj": sixj}


def reference(psi, left_ops, right_ops, source, coef_index, sixj):
    coef = sixj[coef_index]

    def one_sector(s):
        left = left_ops[:, s].astype(jnp.float32)
        right = right_ops[:, s].astype(jnp.float32)
        picked = psi[source[:, s]].astype(jnp.float32)
        half = jnp.einsum("pib,pbc->pic", left, picked).astype(jnp.bfloat16)
        half = lax.optimization_barrier(half).astype(jnp.float32)
        full = jnp.einsum("pic,pjc->pij", half, right)
        return jnp.sum(full * coef[:, s][:, None, None], axis=0)

    total = lax.map(one_sector, jnp.arange(NS))
    return jnp.transpose(total, (1, 0, 2)).astype(jnp.bfloat16)
```

```python
import functools

import jax
import jax.numpy as jnp
from jax import lax
from jax.experimental import pallas as pl
from jax.experimental.pallas import tpu as pltpu
from jax.sharding import PartitionSpec as P

OPG = "opg"
SEC = "sec"
PARTS = 4
NEAR = 2
TILE = 256
KERNEL_VMEM = 24_000_000
PLAN_FLOPS = 20_000_000_000


def flip(x, axis, size, bit):
    return lax.ppermute(x, axis, [(i, i ^ bit) for i in range(size)])


def bits_of(size):
    return [1 << k for k in range(size.bit_length() - 1)]


def tiles(size):
    return [slice(at, min(at + TILE, size)) for at in range(0, size, TILE)]


CLASSES = 3


def make_plan(meta, plan, scale, pairs, local):
    slots = local * pairs
    for kind in range(CLASSES):
        plan[kind, 3 * slots] = 0
    me_sec = lax.axis_index(SEC)

    def sector(s):
        def one(p, carry):
            src = meta[s, p].astype(jnp.int32)
            r, j = lax.div(src, local) ^ me_sec, lax.rem(src, local)
            kind = jnp.where(r < NEAR, 0, 1 + lax.rem(r, 2))
            block = jnp.where(r < NEAR, r, lax.div(r, 2) - 1) * local + j
            n = plan[kind, 3 * slots]
            plan[kind, n] = p
            plan[kind, slots + n] = s
            plan[kind, 2 * slots + n] = block
            scale[kind, n] = meta[local + s, p]
            plan[kind, 3 * slots] = n + 1
            return carry

        lax.fori_loop(0, pairs, one, 0)

    for s in range(local):
        sector(s)


def run(kind, plan, scale, left, right, psi, acc, even, odd):
    pairs, local, sb, _ = left.shape
    slots = local * pairs
    count = plan[kind, 3 * slots]

    def first(i, halves):
        i = jnp.minimum(i, count - 1)
        p, s, block = [plan[kind, k * slots + i] for k in range(3)]
        half = jnp.dot(left[p, s], psi[block], preferred_element_type=jnp.float32)
        halves[...] = (half * scale[kind, i]).astype(jnp.bfloat16)

    def second(i, halves):
        p, s = [plan[kind, k * slots + i] for k in range(2)]
        for c in tiles(sb):
            for k in tiles(sb):
                acc[s, :, c] += lax.dot_general(
                    halves[:, k],
                    right[p, s, c, k],
                    (((1,), (1,)), ((), ())),
                    preferred_element_type=jnp.float32,
                )

    def two(j, carry):
        i = 2 * j
        first(i + 1, odd)
        second(i, even)
        first(i + 2, even)
        second(i + 1, odd)
        return carry

    @pl.when(count > 0)
    def _():
        first(0, even)
        lax.fori_loop(0, lax.div(count, 2), two, 0)

        @pl.when(lax.rem(count, 2) == 1)
        def _():
            second(count - 1, even)


def plan_kernel(local, meta, plan, scale):
    make_plan(meta, plan, scale, meta.shape[1], local)


def products_kernel(kind, n_opg, plan, scale, left, right, *refs):
    local, sb = left.shape[1:3]
    last = kind == CLASSES - 1
    outs = n_opg if last else 1
    pieces, refs = refs[: -outs - 3 - last], refs[-outs - 3 - last :]
    psi, even, odd = refs[outs : outs + 3]
    acc = refs[-1] if last else refs[0]
    if kind:
        acc[...] = pieces[0][...]
        pieces = pieces[1:]
    else:
        acc[...] = jnp.zeros_like(acc)
    if len(pieces) == 1:
        psi = pieces[0]
    else:
        for i, piece in enumerate(pieces):
            psi[i * local : (i + 1) * local] = piece[...]
    run(kind, plan, scale, left, right, psi, acc, even, odd)
    if last:
        me_opg = lax.axis_index(OPG)
        rows = sb // n_opg
        for r, send in enumerate(refs[:outs]):
            at = pl.multiple_of((r ^ me_opg) * rows, 8)
            send[...] = acc[:, pl.ds(at, rows), :].astype(send.dtype)


SMEM = pl.BlockSpec(memory_space=pltpu.SMEM)
VMEM = pl.BlockSpec(memory_space=pltpu.VMEM)


def products(kind, n_opg, plan, scale, left, right, totals, pieces):
    pairs, local, sb, _ = left.shape
    out_shape = jax.ShapeDtypeStruct((local, sb, sb), jnp.float32)
    scratch = []
    if kind == CLASSES - 1:
        scratch = [pltpu.VMEM(out_shape.shape, out_shape.dtype)]
        out_shape = tuple(
            jax.ShapeDtypeStruct(
                (local, sb // n_opg, sb), jnp.bfloat16 if r % PARTS else jnp.float32
            )
            for r in range(n_opg)
        )
    return pl.pallas_call(
        functools.partial(products_kernel, kind, n_opg),
        out_shape=out_shape,
        in_specs=[SMEM] * 2 + [VMEM] * (2 + len(totals) + len(pieces)),
        out_specs=jax.tree.map(lambda _: VMEM, out_shape),
        scratch_shapes=[
            pltpu.VMEM((len(pieces) * local, sb, sb), jnp.bfloat16),
            pltpu.VMEM((sb, sb), jnp.bfloat16),
            pltpu.VMEM((sb, sb), jnp.bfloat16),
            *scratch,
        ],
        compiler_params=pltpu.CompilerParams(vmem_limit_bytes=KERNEL_VMEM),
        cost_estimate=pl.CostEstimate(flops=sb, bytes_accessed=0, transcendentals=0),
    )(plan, scale, left, right, *totals, *pieces)


def scatter_sum(sends, n_opg):
    out = []
    for high in reversed(range(n_opg // PARTS)):
        at = high * PARTS
        total = sends[at]
        for low in (3, 1, 2):
            total = total + flip(sends[at + low], OPG, n_opg, low).astype(jnp.float32)
        if high:
            total = flip(total.astype(jnp.bfloat16), OPG, n_opg, at).astype(jnp.float32)
        out.append(total)
    return sum(out[:-1], out[-1])


def on_device(n_opg, n_sec, psi, left_ops, right_ops, source, coef_index, sixj):
    local = psi.shape[0]
    pairs = left_ops.shape[0]

    twins = {0: psi}
    for bit in bits_of(n_sec)[1:]:
        twins.update({r | bit: flip(x, SEC, n_sec, bit) for r, x in twins.items()})
    twins = [twins[r] for r in range(NEAR, n_sec, 2)]
    partner = flip(psi, SEC, n_sec, 1)

    table = jnp.arange(sixj.shape[0], dtype=jnp.int32)
    coef = jnp.sum(jnp.where(coef_index.T[:, :, None] == table, sixj, 0.0), axis=2)
    meta = jnp.concatenate([source.T.astype(jnp.float32), coef])
    plan, scale = pl.pallas_call(
        functools.partial(plan_kernel, local),
        out_shape=(
            jax.ShapeDtypeStruct((CLASSES, 3 * local * pairs + 1), jnp.int32),
            jax.ShapeDtypeStruct((CLASSES, local * pairs), jnp.float32),
        ),
        in_specs=[SMEM],
        out_specs=(SMEM, SMEM),
        compiler_params=pltpu.CompilerParams(vmem_limit_bytes=KERNEL_VMEM),
        cost_estimate=pl.CostEstimate(flops=PLAN_FLOPS, bytes_accessed=0, transcendentals=0),
    )(meta)

    def onto(kind, totals, pieces):
        return products(kind, n_opg, plan, scale, left_ops, right_ops, totals, pieces)

    done = onto(0, [], [psi, partner])
    twins, done = lax.optimization_barrier((twins, done))
    others = [flip(x, SEC, n_sec, 1) for x in twins]
    done = onto(1, [done], twins)
    sends = onto(2, [done], others)
    return jnp.swapaxes(scatter_sum(sends, n_opg), 0, 1).astype(jnp.bfloat16)


def solution(mesh):
    n_opg, n_sec = mesh.shape[OPG], mesh.shape[SEC]
    placed = (
        P(SEC, None, None),
        P(OPG, SEC, None, None),
        P(OPG, SEC, None, None),
        P(OPG, SEC),
        P(OPG, SEC),
        P(),
    )
    return jax.shard_map(
        functools.partial(on_device, n_opg, n_sec),
        mesh=mesh,
        in_specs=placed,
        out_specs=P(OPG, SEC, None),
        check_vma=False,
    )
```

```python
import functools

import jax
import jax.numpy as jnp
from jax import lax
from jax.experimental import pallas as pl
from jax.experimental.pallas import tpu as pltpu
from jax.sharding import PartitionSpec as P

OPG = "opg"
SEC = "sec"
PARTS = 4
HALVES = 2
NEAR = 2
TILE = 256
KERNEL_VMEM = 24_000_000
PLAN_FLOPS = 20_000_000_000


def flip(x, axis, size, bit):
    return lax.ppermute(x, axis, [(i, i ^ bit) for i in range(size)])


def bits_of(size):
    return [1 << k for k in range(size.bit_length() - 1)]


def tiles(size):
    return [slice(at, min(at + TILE, size)) for at in range(0, size, TILE)]


CLASSES = 3


def make_plan(meta, plan, scale, pairs, local):
    slots = local * pairs
    for kind in range(CLASSES):
        plan[kind, 3 * slots] = 0
    me_sec = lax.axis_index(SEC)

    def sector(s):
        def one(p, carry):
            src = meta[s, p].astype(jnp.int32)
            r, j = lax.div(src, local) ^ me_sec, lax.rem(src, local)
            kind = jnp.where(r < NEAR, 0, 1 + lax.rem(r, 2))
            block = jnp.where(r < NEAR, r, lax.div(r, 2) - 1) * local + j
            n = plan[kind, 3 * slots]
            plan[kind, n] = p
            plan[kind, slots + n] = s
            plan[kind, 2 * slots + n] = block
            scale[kind, n] = meta[local + s, p]
            plan[kind, 3 * slots] = n + 1
            return carry

        lax.fori_loop(0, pairs, one, 0)

    for s in range(local):
        sector(s)


def run(kind, plan, scale, left, right, psi, acc, even, odd):
    pairs, local, sb, _ = left.shape
    slots = local * pairs
    count = plan[kind, 3 * slots]

    def first(i, halves):
        i = jnp.minimum(i, count - 1)
        p, s, block = [plan[kind, k * slots + i] for k in range(3)]
        half = jnp.dot(left[p, s], psi[block], preferred_element_type=jnp.float32)
        halves[...] = (half * scale[kind, i]).astype(jnp.bfloat16)

    def second(i, halves):
        p, s = [plan[kind, k * slots + i] for k in range(2)]
        for c in tiles(sb):
            for k in tiles(sb):
                acc[s, :, c] += lax.dot_general(
                    halves[:, k],
                    right[p, s, c, k],
                    (((1,), (1,)), ((), ())),
                    preferred_element_type=jnp.float32,
                )

    def two(j, carry):
        i = 2 * j
        first(i + 1, odd)
        second(i, even)
        first(i + 2, even)
        second(i + 1, odd)
        return carry

    @pl.when(count > 0)
    def _():
        first(0, even)
        lax.fori_loop(0, lax.div(count, 2), two, 0)

        @pl.when(lax.rem(count, 2) == 1)
        def _():
            second(count - 1, even)


def plan_kernel(local, meta, plan, scale):
    make_plan(meta, plan, scale, meta.shape[1], local)


def products_kernel(kind, n_opg, plan, scale, left, right, *refs):
    local, sb = left.shape[1:3]
    last = kind == CLASSES - 1
    outs = n_opg if last else 1
    pieces, refs = refs[: -outs - 3 - last], refs[-outs - 3 - last :]
    psi, even, odd = refs[outs : outs + 3]
    acc = refs[-1] if last else refs[0]
    if kind:
        acc[...] = pieces[0][...]
        pieces = pieces[1:]
    else:
        acc[...] = jnp.zeros_like(acc)
    if kind == 0:
        for i, piece in enumerate(pieces):
            psi[i * local : (i + 1) * local] = piece[...]
    else:
        half = lax.rem(lax.axis_index(OPG), HALVES)
        rows = sb // HALVES
        for i in range(len(pieces) // 3):
            whole, here, there = pieces[3 * i : 3 * i + 3]
            end = (i + 1) * local - 1
            psi[i * local : end] = whole[...]
            psi[end, pl.ds(pl.multiple_of(half * rows, 16), rows), :] = here[...]
            psi[end, pl.ds(pl.multiple_of((1 - half) * rows, 16), rows), :] = there[...]
    run(kind, plan, scale, left, right, psi, acc, even, odd)
    if last:
        me_opg = lax.axis_index(OPG)
        rows = sb // n_opg
        for r, send in enumerate(refs[:outs]):
            at = pl.multiple_of((r ^ me_opg) * rows, 8)
            send[...] = acc[:, pl.ds(at, rows), :].astype(send.dtype)


SMEM = pl.BlockSpec(memory_space=pltpu.SMEM)
VMEM = pl.BlockSpec(memory_space=pltpu.VMEM)


def products(kind, n_opg, plan, scale, left, right, totals, pieces):
    pairs, local, sb, _ = left.shape
    out_shape = jax.ShapeDtypeStruct((local, sb, sb), jnp.float32)
    scratch = []
    if kind == CLASSES - 1:
        scratch = [pltpu.VMEM(out_shape.shape, out_shape.dtype)]
        out_shape = tuple(
            jax.ShapeDtypeStruct(
                (local, sb // n_opg, sb), jnp.bfloat16 if r % PARTS else jnp.float32
            )
            for r in range(n_opg)
        )
    return pl.pallas_call(
        functools.partial(products_kernel, kind, n_opg),
        out_shape=out_shape,
        in_specs=[SMEM] * 2 + [VMEM] * (2 + len(totals) + len(pieces)),
        out_specs=jax.tree.map(lambda _: VMEM, out_shape),
        scratch_shapes=[
            pltpu.VMEM((len(pieces) // (3 if kind else 1) * local, sb, sb), jnp.bfloat16),
            pltpu.VMEM((sb, sb), jnp.bfloat16),
            pltpu.VMEM((sb, sb), jnp.bfloat16),
            *scratch,
        ],
        compiler_params=pltpu.CompilerParams(vmem_limit_bytes=KERNEL_VMEM),
        cost_estimate=pl.CostEstimate(flops=sb, bytes_accessed=0, transcendentals=0),
    )(plan, scale, left, right, *totals, *pieces)


def scatter_sum(sends, n_opg):
    out = []
    for high in reversed(range(n_opg // PARTS)):
        at = high * PARTS
        total = sends[at]
        for low in (3, 1, 2):
            total = total + flip(sends[at + low], OPG, n_opg, low).astype(jnp.float32)
        if high:
            total = flip(total.astype(jnp.bfloat16), OPG, n_opg, at).astype(jnp.float32)
        out.append(total)
    return sum(out[:-1], out[-1])


def on_device(n_opg, n_sec, psi, left_ops, right_ops, source, coef_index, sixj):
    local, sb, _ = psi.shape
    pairs = left_ops.shape[0]

    half = lax.rem(lax.axis_index(OPG), HALVES)
    cut = psi[local - 1].reshape(HALVES, sb // HALVES, sb)
    here = {0: lax.dynamic_index_in_dim(cut, half, axis=0, keepdims=False)}
    whole = {0: psi[: local - 1]}
    for bit in bits_of(n_sec)[1:]:
        for held in (here, whole):
            held.update({r | bit: flip(x, SEC, n_sec, bit) for r, x in held.items()})
    far = range(NEAR, n_sec, 2)
    here, whole = [here[r] for r in far], [whole[r] for r in far]
    partner = flip(psi, SEC, n_sec, 1)

    table = jnp.arange(sixj.shape[0], dtype=jnp.int32)
    coef = jnp.sum(jnp.where(coef_index.T[:, :, None] == table, sixj, 0.0), axis=2)
    meta = jnp.concatenate([source.T.astype(jnp.float32), coef])
    plan, scale = pl.pallas_call(
        functools.partial(plan_kernel, local),
        out_shape=(
            jax.ShapeDtypeStruct((CLASSES, 3 * local * pairs + 1), jnp.int32),
            jax.ShapeDtypeStruct((CLASSES, local * pairs), jnp.float32),
        ),
        in_specs=[SMEM],
        out_specs=(SMEM, SMEM),
        compiler_params=pltpu.CompilerParams(vmem_limit_bytes=KERNEL_VMEM),
        cost_estimate=pl.CostEstimate(flops=PLAN_FLOPS, bytes_accessed=0, transcendentals=0),
    )(meta)

    def onto(kind, totals, pieces):
        return products(kind, n_opg, plan, scale, left_ops, right_ops, totals, pieces)

    def to_other_core(pieces):
        return [flip(x, SEC, n_sec, 1) for x in pieces]

    here, plan, scale = lax.optimization_barrier((here, plan, scale))
    there = [flip(x, OPG, n_opg, 1) for x in here]
    here_crossed = to_other_core(here)
    done = onto(0, [], [psi, partner])
    there, whole, here_crossed, done = lax.optimization_barrier((there, whole, here_crossed, done))
    there_crossed, whole_crossed = to_other_core(there), to_other_core(whole)
    done = onto(1, [done], [x for three in zip(whole, here, there) for x in three])
    crossed = zip(whole_crossed, here_crossed, there_crossed)
    sends = onto(2, [done], [x for three in crossed for x in three])
    return jnp.swapaxes(scatter_sum(sends, n_opg), 0, 1).astype(jnp.bfloat16)


def solution(mesh):
    n_opg, n_sec = mesh.shape[OPG], mesh.shape[SEC]
    placed = (
        P(SEC, None, None),
        P(OPG, SEC, None, None),
        P(OPG, SEC, None, None),
        P(OPG, SEC),
        P(OPG, SEC),
        P(),
    )
    return jax.shard_map(
        functools.partial(on_device, n_opg, n_sec),
        mesh=mesh,
        in_specs=placed,
        out_specs=P(OPG, SEC, None),
        check_vma=False,
    )
```

```python
import functools

import jax
import jax.numpy as jnp
from jax import lax
from jax.experimental import pallas as pl
from jax.experimental.pallas import tpu as pltpu
from jax.sharding import PartitionSpec as P

OPG = "opg"
SEC = "sec"
PARTS = 4
HALVES = 2
NEAR = 2
TILE = 256
KERNEL_VMEM = 24_000_000
PLAN_FLOPS = 20_000_000_000


def flip(x, axis, size, bit):
    return lax.ppermute(x, axis, [(i, i ^ bit) for i in range(size)])


def bits_of(size):
    return [1 << k for k in range(size.bit_length() - 1)]


def tiles(size):
    return [slice(at, min(at + TILE, size)) for at in range(0, size, TILE)]


CLASSES = 3


def make_plan(meta, plan, pairs, local):
    slots = local * pairs
    me_sec = lax.axis_index(SEC)
    for kind in range(CLASSES):
        for k in range(local + 1):
            plan[kind, 4 * slots + k] = 0.0

    def sector(s):
        def one(p, carry):
            src = meta[s, p].astype(jnp.int32)
            r, j = lax.div(src, local) ^ me_sec, lax.rem(src, local)
            kind = jnp.where(r < NEAR, 0, 1 + lax.rem(r, 2))
            block = jnp.where(r < NEAR, r, lax.div(r, 2) - 1) * local + j
            count = plan[kind, 4 * slots + local]
            n = count.astype(jnp.int32)
            plan[kind, n] = p.astype(jnp.float32)
            plan[kind, slots + n] = float(s)
            plan[kind, 2 * slots + n] = block.astype(jnp.float32)
            plan[kind, 3 * slots + n] = meta[local + s, p]
            plan[kind, 4 * slots + s] += 1.0
            plan[kind, 4 * slots + local] = count + 1.0
            return carry

        lax.fori_loop(0, pairs, one, 0)

    for s in range(local):
        sector(s)


def run(kind, plan, left, right, psi, total, acc, even, odd):
    pairs, local, sb, _ = left.shape
    slots = local * pairs
    count = plan[kind, 4 * slots + local].astype(jnp.int32)

    def entry(k, i):
        return plan[kind, k * slots + i].astype(jnp.int32)

    def start(s, c):
        return jnp.zeros((sb, c.stop - c.start), acc.dtype) if total is None else total[s, :, c]

    def first(i, halves):
        i = jnp.minimum(i, count - 1)
        p, s, block = [entry(k, i) for k in range(3)]
        half = jnp.dot(left[p, s], psi[block], preferred_element_type=jnp.float32)
        halves[...] = (half * plan[kind, 3 * slots + i]).astype(jnp.bfloat16)

    def second(i, halves):
        p, s = [entry(k, i) for k in range(2)]
        fresh = (i == 0) | (entry(1, jnp.maximum(i - 1, 0)) != s)
        for c in tiles(sb):
            for k in tiles(sb):
                term = lax.dot_general(
                    halves[:, k],
                    right[p, s, c, k],
                    (((1,), (1,)), ((), ())),
                    preferred_element_type=jnp.float32,
                )
                if k.start == 0:
                    acc[s, :, c] = jnp.where(fresh, start(s, c), acc[s, :, c]) + term
                else:
                    acc[s, :, c] += term

    def two(j, carry):
        i = 2 * j
        first(i + 1, odd)
        second(i, even)
        first(i + 2, even)
        second(i + 1, odd)
        return carry

    for s in range(local):

        @pl.when(plan[kind, 4 * slots + s] == 0.0)
        def _():
            acc[s] = start(s, slice(0, sb))

    @pl.when(count > 0)
    def _():
        first(0, even)
        lax.fori_loop(0, lax.div(count, 2), two, 0)

        @pl.when(lax.rem(count, 2) == 1)
        def _():
            second(count - 1, even)


def plan_kernel(local, meta, plan):
    make_plan(meta, plan, meta.shape[1], local)


def products_kernel(kind, n_opg, plan, left, right, *refs):
    local, sb = left.shape[1:3]
    last = kind == CLASSES - 1
    outs = n_opg if last else 1
    pieces, refs = refs[: -outs - 3 - last], refs[-outs - 3 - last :]
    psi, even, odd = refs[outs : outs + 3]
    acc = refs[-1] if last else refs[0]
    total, pieces = (pieces[0], pieces[1:]) if kind else (None, pieces)
    if kind == 0:
        for i, piece in enumerate(pieces):
            psi[i * local : (i + 1) * local] = piece[...]
    else:
        half = lax.rem(lax.axis_index(OPG), HALVES)
        rows = sb // HALVES
        for i in range(len(pieces) // 3):
            whole, here, there = pieces[3 * i : 3 * i + 3]
            end = (i + 1) * local - 1
            psi[i * local : end] = whole[...]
            psi[end, pl.ds(pl.multiple_of(half * rows, 16), rows), :] = here[...]
            psi[end, pl.ds(pl.multiple_of((1 - half) * rows, 16), rows), :] = there[...]
    run(kind, plan, left, right, psi, total, acc, even, odd)
    if last:
        me_opg = lax.axis_index(OPG)
        rows = sb // n_opg
        for r, send in enumerate(refs[:outs]):
            at = pl.multiple_of((r ^ me_opg) * rows, 8)
            send[...] = acc[:, pl.ds(at, rows), :].astype(send.dtype)


SMEM = pl.BlockSpec(memory_space=pltpu.SMEM)
VMEM = pl.BlockSpec(memory_space=pltpu.VMEM)


def products(kind, n_opg, plan, left, right, totals, pieces):
    pairs, local, sb, _ = left.shape
    out_shape = jax.ShapeDtypeStruct((local, sb, sb), jnp.float32)
    scratch = []
    if kind == CLASSES - 1:
        scratch = [pltpu.VMEM(out_shape.shape, out_shape.dtype)]
        out_shape = tuple(
            jax.ShapeDtypeStruct(
                (local, sb // n_opg, sb), jnp.bfloat16 if r % PARTS else jnp.float32
            )
            for r in range(n_opg)
        )
    return pl.pallas_call(
        functools.partial(products_kernel, kind, n_opg),
        out_shape=out_shape,
        in_specs=[SMEM] + [VMEM] * (2 + len(totals) + len(pieces)),
        out_specs=jax.tree.map(lambda _: VMEM, out_shape),
        scratch_shapes=[
            pltpu.VMEM((len(pieces) // (3 if kind else 1) * local, sb, sb), jnp.bfloat16),
            pltpu.VMEM((sb, sb), jnp.bfloat16),
            pltpu.VMEM((sb, sb), jnp.bfloat16),
            *scratch,
        ],
        compiler_params=pltpu.CompilerParams(vmem_limit_bytes=KERNEL_VMEM),
        cost_estimate=pl.CostEstimate(flops=sb, bytes_accessed=0, transcendentals=0),
    )(plan, left, right, *totals, *pieces)


def scatter_sum(sends, n_opg):
    out = []
    for high in reversed(range(n_opg // PARTS)):
        at = high * PARTS
        total = sends[at]
        for low in (3, 1, 2):
            total = total + flip(sends[at + low], OPG, n_opg, low).astype(jnp.float32)
        if high:
            total = flip(total.astype(jnp.bfloat16), OPG, n_opg, at).astype(jnp.float32)
        out.append(total)
    return sum(out[:-1], out[-1])


def on_device(n_opg, n_sec, psi, left_ops, right_ops, source, coef_index, sixj):
    local, sb, _ = psi.shape
    pairs = left_ops.shape[0]

    half = lax.rem(lax.axis_index(OPG), HALVES)
    rows = sb // HALVES
    ours = lax.dynamic_slice(psi, (local - 1, half * rows, 0), (1, rows, sb))[0]
    ours, psi = lax.optimization_barrier((ours, psi))
    here = {0: ours}
    whole = {0: psi[: local - 1]}
    for bit in bits_of(n_sec)[1:]:
        for held in (here, whole):
            held.update({r | bit: flip(x, SEC, n_sec, bit) for r, x in held.items()})
    far = range(NEAR, n_sec, 2)
    here, whole = [here[r] for r in far], [whole[r] for r in far]
    partner = flip(psi, SEC, n_sec, 1)

    table = jnp.arange(sixj.shape[0], dtype=jnp.int32)
    coef = jnp.sum(jnp.where(coef_index.T[:, :, None] == table, sixj, 0.0), axis=2)
    meta = jnp.concatenate([source.T.astype(jnp.float32), coef])
    plan = pl.pallas_call(
        functools.partial(plan_kernel, local),
        out_shape=jax.ShapeDtypeStruct((CLASSES, 4 * local * pairs + local + 1), jnp.float32),
        in_specs=[SMEM],
        out_specs=SMEM,
        compiler_params=pltpu.CompilerParams(vmem_limit_bytes=KERNEL_VMEM),
        cost_estimate=pl.CostEstimate(flops=PLAN_FLOPS, bytes_accessed=0, transcendentals=0),
    )(meta)

    def onto(kind, totals, pieces):
        return products(kind, n_opg, plan, left_ops, right_ops, totals, pieces)

    def to_other_core(pieces):
        return [flip(x, SEC, n_sec, 1) for x in pieces]

    here, plan = lax.optimization_barrier((here, plan))
    there = [flip(x, OPG, n_opg, 1) for x in here]
    here_crossed = to_other_core(here)
    done = onto(0, [], [psi, partner])
    there, whole, here_crossed, done = lax.optimization_barrier((there, whole, here_crossed, done))
    there_crossed, whole_crossed = to_other_core(there), to_other_core(whole)
    done = onto(1, [done], [x for three in zip(whole, here, there) for x in three])
    crossed = zip(whole_crossed, here_crossed, there_crossed)
    sends = onto(2, [done], [x for three in crossed for x in three])
    return jnp.swapaxes(scatter_sum(sends, n_opg), 0, 1).astype(jnp.bfloat16)


def solution(mesh):
    n_opg, n_sec = mesh.shape[OPG], mesh.shape[SEC]
    placed = (
        P(SEC, None, None),
        P(OPG, SEC, None, None),
        P(OPG, SEC, None, None),
        P(OPG, SEC),
        P(OPG, SEC),
        P(),
    )
    return jax.shard_map(
        functools.partial(on_device, n_opg, n_sec),
        mesh=mesh,
        in_specs=placed,
        out_specs=P(OPG, SEC, None),
        check_vma=False,
    )
```

```python
import functools

import jax
import jax.numpy as jnp
from jax import lax
from jax.experimental import pallas as pl
from jax.experimental.pallas import tpu as pltpu
from jax.sharding import PartitionSpec as P

OPG = "opg"
SEC = "sec"
PARTS = 4
HALVES = 2
NEAR = 2
KERNEL_VMEM = 24_000_000
PLAN_FLOPS = 20_000_000_000


def flip(x, axis, size, bit):
    return lax.ppermute(x, axis, [(i, i ^ bit) for i in range(size)])


def bits_of(size):
    return [1 << k for k in range(size.bit_length() - 1)]


CLASSES = 3


def make_plan(meta, plan, scale, pairs, local):
    slots = local * pairs
    for kind in range(CLASSES):
        plan[kind, 3 * slots] = 0
    me_sec = lax.axis_index(SEC)

    def sector(s):
        def one(p, carry):
            src = meta[s, p].astype(jnp.int32)
            r, j = lax.div(src, local) ^ me_sec, lax.rem(src, local)
            kind = jnp.where(r < NEAR, 0, 1 + lax.rem(r, 2))
            block = jnp.where(r < NEAR, r, lax.div(r, 2) - 1) * local + j
            n = plan[kind, 3 * slots]
            plan[kind, n] = p
            plan[kind, slots + n] = s
            plan[kind, 2 * slots + n] = block
            scale[kind, n] = meta[local + s, p]
            plan[kind, 3 * slots] = n + 1
            return carry

        lax.fori_loop(0, pairs, one, 0)

    for s in range(local):
        sector(s)


def thirds(x, w, transposed):
    size = x.shape[1] // 3
    cut = [slice(i * size, (i + 1) * size) for i in range(3)]
    none = jnp.zeros((size, size), w.dtype)

    def tile(depth, columns, absent):
        def block(k, n):
            if (k, n) in absent:
                return none
            return w[cut[n], cut[k]] if transposed else w[cut[k], cut[n]]

        one, two = (columns, depth) if transposed else (depth, columns)
        rows = [
            jnp.concatenate(
                [block(j, i) if transposed else block(i, j) for j in two], axis=1
            )
            for i in one
        ]
        return jnp.concatenate(rows, axis=0)

    def product(depth, columns, absent):
        return lax.dot_general(
            jnp.concatenate([x[:, cut[k]] for k in depth], axis=1),
            tile(depth, columns, absent),
            (((1,), (1 if transposed else 0,)), ((), ())),
            preferred_element_type=jnp.float32,
        )

    p = product((0, 1), (0, 1), ())
    q = product((0, 2), (2, 0), ((0, 0),))
    r = product((1, 2), (2, 1), ((1, 1), (2, 2)))
    low, high = slice(0, size), slice(size, 2 * size)
    return list(zip(cut, (p[:, low] + q[:, high], p[:, high] + r[:, high], q[:, low] + r[:, low])))


def run(kind, plan, scale, left, right, psi, acc, even, odd):
    pairs, local = left.shape[:2]
    slots = local * pairs
    count = plan[kind, 3 * slots]

    def first(i, halves):
        i = jnp.minimum(i, count - 1)
        p, s, block = [plan[kind, k * slots + i] for k in range(3)]
        for c, half in thirds(left.at[p, s], psi.at[block], False):
            halves[:, c] = (half * scale[kind, i]).astype(jnp.bfloat16)

    def second(i, halves):
        p, s = [plan[kind, k * slots + i] for k in range(2)]
        for c, term in thirds(halves, right.at[p, s], True):
            acc[s, :, c] += term

    def two(j, carry):
        i = 2 * j
        first(i + 1, odd)
        second(i, even)
        first(i + 2, even)
        second(i + 1, odd)
        return carry

    @pl.when(count > 0)
    def _():
        first(0, even)
        lax.fori_loop(0, lax.div(count, 2), two, 0)

        @pl.when(lax.rem(count, 2) == 1)
        def _():
            second(count - 1, even)


def plan_kernel(local, meta, plan, scale):
    make_plan(meta, plan, scale, meta.shape[1], local)


def products_kernel(kind, n_opg, plan, scale, left, right, *refs):
    local, sb = left.shape[1:3]
    last = kind == CLASSES - 1
    outs = n_opg if last else 1
    pieces, refs = refs[: -outs - 3 - last], refs[-outs - 3 - last :]
    psi, even, odd = refs[outs : outs + 3]
    acc = refs[-1] if last else refs[0]
    if kind:
        acc[...] = pieces[0][...]
        pieces = pieces[1:]
    else:
        acc[...] = jnp.zeros_like(acc)
    if kind == 0:
        for i, piece in enumerate(pieces):
            psi[i * local : (i + 1) * local] = piece[...]
    else:
        half = lax.rem(lax.axis_index(OPG), HALVES)
        rows = sb // HALVES
        for i in range(len(pieces) // 3):
            whole, here, there = pieces[3 * i : 3 * i + 3]
            end = (i + 1) * local - 1
            psi[i * local : end] = whole[...]
            psi[end, pl.ds(pl.multiple_of(half * rows, 16), rows), :] = here[...]
            psi[end, pl.ds(pl.multiple_of((1 - half) * rows, 16), rows), :] = there[...]
    run(kind, plan, scale, left, right, psi, acc, even, odd)
    if last:
        me_opg = lax.axis_index(OPG)
        rows = sb // n_opg
        for r, send in enumerate(refs[:outs]):
            at = pl.multiple_of((r ^ me_opg) * rows, 8)
            send[...] = acc[:, pl.ds(at, rows), :].astype(send.dtype)


SMEM = pl.BlockSpec(memory_space=pltpu.SMEM)
VMEM = pl.BlockSpec(memory_space=pltpu.VMEM)


def products(kind, n_opg, plan, scale, left, right, totals, pieces):
    pairs, local, sb, _ = left.shape
    out_shape = jax.ShapeDtypeStruct((local, sb, sb), jnp.float32)
    scratch = []
    if kind == CLASSES - 1:
        scratch = [pltpu.VMEM(out_shape.shape, out_shape.dtype)]
        out_shape = tuple(
            jax.ShapeDtypeStruct(
                (local, sb // n_opg, sb), jnp.bfloat16 if r % PARTS else jnp.float32
            )
            for r in range(n_opg)
        )
    return pl.pallas_call(
        functools.partial(products_kernel, kind, n_opg),
        out_shape=out_shape,
        in_specs=[SMEM] * 2 + [VMEM] * (2 + len(totals) + len(pieces)),
        out_specs=jax.tree.map(lambda _: VMEM, out_shape),
        scratch_shapes=[
            pltpu.VMEM((len(pieces) // (3 if kind else 1) * local, sb, sb), jnp.bfloat16),
            pltpu.VMEM((sb, sb), jnp.bfloat16),
            pltpu.VMEM((sb, sb), jnp.bfloat16),
            *scratch,
        ],
        compiler_params=pltpu.CompilerParams(vmem_limit_bytes=KERNEL_VMEM),
        cost_estimate=pl.CostEstimate(flops=sb, bytes_accessed=0, transcendentals=0),
    )(plan, scale, left, right, *totals, *pieces)


def scatter_sum(sends, n_opg):
    out = []
    for high in reversed(range(n_opg // PARTS)):
        at = high * PARTS
        total = sends[at]
        for low in (3, 1, 2):
            total = total + flip(sends[at + low], OPG, n_opg, low).astype(jnp.float32)
        if high:
            total = flip(total.astype(jnp.bfloat16), OPG, n_opg, at).astype(jnp.float32)
        out.append(total)
    return sum(out[:-1], out[-1])


def on_device(n_opg, n_sec, psi, left_ops, right_ops, source, coef_index, sixj):
    local, sb, _ = psi.shape
    pairs = left_ops.shape[0]

    half = lax.rem(lax.axis_index(OPG), HALVES)
    cut = psi[local - 1].reshape(HALVES, sb // HALVES, sb)
    here = {0: lax.dynamic_index_in_dim(cut, half, axis=0, keepdims=False)}
    whole = {0: psi[: local - 1]}
    for bit in bits_of(n_sec)[1:]:
        for held in (here, whole):
            held.update({r | bit: flip(x, SEC, n_sec, bit) for r, x in held.items()})
    far = range(NEAR, n_sec, 2)
    here, whole = [here[r] for r in far], [whole[r] for r in far]
    partner = flip(psi, SEC, n_sec, 1)

    table = jnp.arange(sixj.shape[0], dtype=jnp.int32)
    coef = jnp.sum(jnp.where(coef_index.T[:, :, None] == table, sixj, 0.0), axis=2)
    meta = jnp.concatenate([source.T.astype(jnp.float32), coef])
    plan, scale = pl.pallas_call(
        functools.partial(plan_kernel, local),
        out_shape=(
            jax.ShapeDtypeStruct((CLASSES, 3 * local * pairs + 1), jnp.int32),
            jax.ShapeDtypeStruct((CLASSES, local * pairs), jnp.float32),
        ),
        in_specs=[SMEM],
        out_specs=(SMEM, SMEM),
        compiler_params=pltpu.CompilerParams(vmem_limit_bytes=KERNEL_VMEM),
        cost_estimate=pl.CostEstimate(flops=PLAN_FLOPS, bytes_accessed=0, transcendentals=0),
    )(meta)

    def onto(kind, totals, pieces):
        return products(kind, n_opg, plan, scale, left_ops, right_ops, totals, pieces)

    def to_other_core(pieces):
        return [flip(x, SEC, n_sec, 1) for x in pieces]

    here, plan, scale = lax.optimization_barrier((here, plan, scale))
    there = [flip(x, OPG, n_opg, 1) for x in here]
    here_crossed = to_other_core(here)
    done = onto(0, [], [psi, partner])
    there, whole, here_crossed, done = lax.optimization_barrier((there, whole, here_crossed, done))
    there_crossed, whole_crossed = to_other_core(there), to_other_core(whole)
    done = onto(1, [done], [x for three in zip(whole, here, there) for x in three])
    crossed = zip(whole_crossed, here_crossed, there_crossed)
    sends = onto(2, [done], [x for three in crossed for x in three])
    return jnp.swapaxes(scatter_sum(sends, n_opg), 0, 1).astype(jnp.bfloat16)


def solution(mesh):
    n_opg, n_sec = mesh.shape[OPG], mesh.shape[SEC]
    placed = (
        P(SEC, None, None),
        P(OPG, SEC, None, None),
        P(OPG, SEC, None, None),
        P(OPG, SEC),
        P(OPG, SEC),
        P(),
    )
    return jax.shard_map(
        functools.partial(on_device, n_opg, n_sec),
        mesh=mesh,
        in_specs=placed,
        out_specs=P(OPG, SEC, None),
        check_vma=False,
    )
```

```python
import functools

import jax
import jax.numpy as jnp
from jax import lax
from jax.experimental import pallas as pl
from jax.experimental.pallas import tpu as pltpu
from jax.sharding import PartitionSpec as P

OPG = "opg"
SEC = "sec"
PARTS = 4
HALVES = 2
NEAR = 2
KERNEL_VMEM = 24_000_000
PLAN_FLOPS = 20_000_000_000


def flip(x, axis, size, bit):
    return lax.ppermute(x, axis, [(i, i ^ bit) for i in range(size)])


def bits_of(size):
    return [1 << k for k in range(size.bit_length() - 1)]


CLASSES = 3


def make_plan(meta, plan, scale, pairs, local):
    slots = local * pairs
    for kind in range(CLASSES):
        plan[kind, 3 * slots] = 0
    me_sec = lax.axis_index(SEC)

    def sector(s):
        def one(p, carry):
            src = meta[s, p].astype(jnp.int32)
            r, j = lax.div(src, local) ^ me_sec, lax.rem(src, local)
            kind = jnp.where(r < NEAR, 0, 1 + lax.rem(r, 2))
            block = jnp.where(r < NEAR, r, lax.div(r, 2) - 1) * local + j
            n = plan[kind, 3 * slots]
            plan[kind, n] = p
            plan[kind, slots + n] = s
            plan[kind, 2 * slots + n] = block
            scale[kind, n] = meta[local + s, p]
            plan[kind, 3 * slots] = n + 1
            return carry

        lax.fori_loop(0, pairs, one, 0)

    for s in range(local):
        sector(s)


def thirds(x, w, transposed):
    size = x.shape[1] // 3
    cut = [slice(i * size, (i + 1) * size) for i in range(3)]
    none = jnp.zeros((size, size), w.dtype)

    def tile(depth, columns, absent):
        def block(k, n):
            if (k, n) in absent:
                return none
            return w[cut[n], cut[k]] if transposed else w[cut[k], cut[n]]

        one, two = (columns, depth) if transposed else (depth, columns)
        rows = [
            jnp.concatenate(
                [block(j, i) if transposed else block(i, j) for j in two], axis=1
            )
            for i in one
        ]
        return jnp.concatenate(rows, axis=0)

    def product(depth, columns, absent):
        return lax.dot_general(
            jnp.concatenate([x[:, cut[k]] for k in depth], axis=1),
            tile(depth, columns, absent),
            (((1,), (1 if transposed else 0,)), ((), ())),
            preferred_element_type=jnp.float32,
        )

    p = product((0, 1), (0, 1), ())
    q = product((0, 2), (2, 0), ((0, 0),))
    r = product((1, 2), (2, 1), ((1, 1), (2, 2)))
    low, high = slice(0, size), slice(size, 2 * size)
    return list(zip(cut, (p[:, low] + q[:, high], p[:, high] + r[:, high], q[:, low] + r[:, low])))


def run(kind, plan, scale, left, right, psi, acc, even, odd):
    pairs, local = left.shape[:2]
    slots = local * pairs
    count = plan[kind, 3 * slots]

    def first(i, halves):
        i = jnp.minimum(i, count - 1)
        p, s, block = [plan[kind, k * slots + i] for k in range(3)]
        for c, half in thirds(left.at[p, s], psi.at[block], False):
            halves[:, c] = (half * scale[kind, i]).astype(jnp.bfloat16)

    def second(i, halves):
        p, s = [plan[kind, k * slots + i] for k in range(2)]
        for c, term in thirds(halves, right.at[p, s], True):
            acc[s, :, c] += term

    def two(j, carry):
        i = 2 * j
        first(i + 1, odd)
        second(i, even)
        first(i + 2, even)
        second(i + 1, odd)
        return carry

    @pl.when(count > 0)
    def _():
        first(0, even)
        lax.fori_loop(0, lax.div(count, 2), two, 0)

        @pl.when(lax.rem(count, 2) == 1)
        def _():
            second(count - 1, even)


def plan_kernel(local, meta, plan, scale):
    make_plan(meta, plan, scale, meta.shape[1], local)


def products_kernel(kind, n_opg, plan, scale, left, right, *refs):
    local, sb = left.shape[1:3]
    last = kind == CLASSES - 1
    outs = n_opg if last else 1
    pieces, refs = refs[: -outs - 3 - last], refs[-outs - 3 - last :]
    psi, even, odd = refs[outs : outs + 3]
    acc = refs[-1] if last else refs[0]
    if kind:
        acc[...] = pieces[0][...]
        pieces = pieces[1:]
    else:
        acc[...] = jnp.zeros_like(acc)
    if kind == 0:
        for i, piece in enumerate(pieces):
            psi[i * local : (i + 1) * local] = piece[...]
    else:
        half = lax.rem(lax.axis_index(OPG), HALVES)
        rows = sb // HALVES
        for i in range(len(pieces) // 2):
            whole, halves = pieces[2 * i : 2 * i + 2]
            end = (i + 1) * local - 1
            psi[i * local : end] = whole[...]
            psi[end, pl.ds(pl.multiple_of(half * rows, 16), rows), :] = halves[0]
            psi[end, pl.ds(pl.multiple_of((1 - half) * rows, 16), rows), :] = halves[1]
    run(kind, plan, scale, left, right, psi, acc, even, odd)
    if last:
        me_opg = lax.axis_index(OPG)
        rows = sb // n_opg
        for r, send in enumerate(refs[:outs]):
            at = pl.multiple_of((r ^ me_opg) * rows, 8)
            send[...] = acc[:, pl.ds(at, rows), :].astype(send.dtype)


SMEM = pl.BlockSpec(memory_space=pltpu.SMEM)
VMEM = pl.BlockSpec(memory_space=pltpu.VMEM)


def products(kind, n_opg, plan, scale, left, right, totals, pieces):
    pairs, local, sb, _ = left.shape
    out_shape = jax.ShapeDtypeStruct((local, sb, sb), jnp.float32)
    scratch = []
    if kind == CLASSES - 1:
        scratch = [pltpu.VMEM(out_shape.shape, out_shape.dtype)]
        out_shape = tuple(
            jax.ShapeDtypeStruct(
                (local, sb // n_opg, sb), jnp.bfloat16 if r % PARTS else jnp.float32
            )
            for r in range(n_opg)
        )
    return pl.pallas_call(
        functools.partial(products_kernel, kind, n_opg),
        out_shape=out_shape,
        in_specs=[SMEM] * 2 + [VMEM] * (2 + len(totals) + len(pieces)),
        out_specs=jax.tree.map(lambda _: VMEM, out_shape),
        scratch_shapes=[
            pltpu.VMEM((len(pieces) // (2 if kind else 1) * local, sb, sb), jnp.bfloat16),
            pltpu.VMEM((sb, sb), jnp.bfloat16),
            pltpu.VMEM((sb, sb), jnp.bfloat16),
            *scratch,
        ],
        compiler_params=pltpu.CompilerParams(vmem_limit_bytes=KERNEL_VMEM),
        cost_estimate=pl.CostEstimate(flops=sb, bytes_accessed=0, transcendentals=0),
    )(plan, scale, left, right, *totals, *pieces)


def scatter_sum(sends, n_opg):
    out = []
    for high in reversed(range(n_opg // PARTS)):
        at = high * PARTS
        total = sends[at]
        for low in (3, 1, 2):
            total = total + flip(sends[at + low], OPG, n_opg, low).astype(jnp.float32)
        if high:
            total = flip(total.astype(jnp.bfloat16), OPG, n_opg, at).astype(jnp.float32)
        out.append(total)
    return sum(out[:-1], out[-1])


def on_device(n_opg, n_sec, psi, left_ops, right_ops, source, coef_index, sixj):
    local, sb, _ = psi.shape
    pairs = left_ops.shape[0]

    half = lax.rem(lax.axis_index(OPG), HALVES)
    cut = psi[local - 1].reshape(HALVES, sb // HALVES, sb)
    ours = lax.dynamic_index_in_dim(cut, half, axis=0, keepdims=False)
    ours, rest, psi = lax.optimization_barrier((ours, psi[: local - 1], psi))
    here, whole = {0: ours}, {0: rest}
    for bit in bits_of(n_sec)[1:]:
        for held in (here, whole):
            held.update({r | bit: flip(x, SEC, n_sec, bit) for r, x in held.items()})
    far = range(NEAR, n_sec, 2)
    here, whole = [here[r] for r in far], [whole[r] for r in far]
    partner = flip(psi, SEC, n_sec, 1)

    table = jnp.arange(sixj.shape[0], dtype=jnp.int32)
    coef = jnp.sum(jnp.where(coef_index.T[:, :, None] == table, sixj, 0.0), axis=2)
    meta = jnp.concatenate([source.T.astype(jnp.float32), coef])
    plan, scale = pl.pallas_call(
        functools.partial(plan_kernel, local),
        out_shape=(
            jax.ShapeDtypeStruct((CLASSES, 3 * local * pairs + 1), jnp.int32),
            jax.ShapeDtypeStruct((CLASSES, local * pairs), jnp.float32),
        ),
        in_specs=[SMEM],
        out_specs=(SMEM, SMEM),
        compiler_params=pltpu.CompilerParams(vmem_limit_bytes=KERNEL_VMEM),
        cost_estimate=pl.CostEstimate(flops=PLAN_FLOPS, bytes_accessed=0, transcendentals=0),
    )(meta)

    def onto(kind, totals, pieces):
        return products(kind, n_opg, plan, scale, left_ops, right_ops, totals, pieces)

    def to_other_core(pieces):
        return [flip(x, SEC, n_sec, 1) for x in pieces]

    here, plan, scale = lax.optimization_barrier((here, plan, scale))
    there = [flip(x, OPG, n_opg, 1) for x in here]
    done = onto(0, [], [psi, partner])
    here, there, whole, done = lax.optimization_barrier((here, there, whole, done))
    whole_crossed = to_other_core(whole)
    halves = [jnp.stack(two) for two in zip(here, there)]
    halves_crossed = to_other_core(halves)
    done = onto(1, [done], [x for two in zip(whole, halves) for x in two])
    sends = onto(2, [done], [x for two in zip(whole_crossed, halves_crossed) for x in two])
    return jnp.swapaxes(scatter_sum(sends, n_opg), 0, 1).astype(jnp.bfloat16)


def solution(mesh):
    n_opg, n_sec = mesh.shape[OPG], mesh.shape[SEC]
    placed = (
        P(SEC, None, None),
        P(OPG, SEC, None, None),
        P(OPG, SEC, None, None),
        P(OPG, SEC),
        P(OPG, SEC),
        P(),
    )
    return jax.shard_map(
        functools.partial(on_device, n_opg, n_sec),
        mesh=mesh,
        in_specs=placed,
        out_specs=P(OPG, SEC, None),
        check_vma=False,
    )
```

```python
import functools

import jax
import jax.numpy as jnp
from jax import lax
from jax.experimental import pallas as pl
from jax.experimental.pallas import tpu as pltpu
from jax.sharding import PartitionSpec as P

OPG = "opg"
SEC = "sec"
PARTS = 4
HALVES = 2
NEAR = 2
KERNEL_VMEM = 24_000_000
PLAN_FLOPS = 20_000_000_000


def flip(x, axis, size, bit):
    return lax.ppermute(x, axis, [(i, i ^ bit) for i in range(size)])


def bits_of(size):
    return [1 << k for k in range(size.bit_length() - 1)]


CLASSES = 3


def make_plan(source, plan, pairs, local):
    slots = local * pairs
    for kind in range(CLASSES):
        plan[kind, 3 * slots] = 0
    me_sec = lax.axis_index(SEC)

    def sector(s):
        def one(p, carry):
            src = source[s, p]
            r, j = lax.div(src, local) ^ me_sec, lax.rem(src, local)
            kind = jnp.where(r < NEAR, 0, 1 + lax.rem(r, 2))
            block = jnp.where(r < NEAR, r, lax.div(r, 2) - 1) * local + j
            n = plan[kind, 3 * slots]
            plan[kind, n] = p
            plan[kind, slots + n] = s
            plan[kind, 2 * slots + n] = block
            plan[kind, 3 * slots] = n + 1
            return carry

        lax.fori_loop(0, pairs, one, 0)

    for s in range(local):
        sector(s)


def thirds(x, w, transposed):
    size = x.shape[1] // 3
    cut = [slice(i * size, (i + 1) * size) for i in range(3)]
    none = jnp.zeros((size, size), w.dtype)

    def tile(depth, columns, absent):
        def block(k, n):
            if (k, n) in absent:
                return none
            return w[cut[n], cut[k]] if transposed else w[cut[k], cut[n]]

        one, two = (columns, depth) if transposed else (depth, columns)
        rows = [
            jnp.concatenate(
                [block(j, i) if transposed else block(i, j) for j in two], axis=1
            )
            for i in one
        ]
        return jnp.concatenate(rows, axis=0)

    def product(depth, columns, absent):
        return lax.dot_general(
            jnp.concatenate([x[:, cut[k]] for k in depth], axis=1),
            tile(depth, columns, absent),
            (((1,), (1 if transposed else 0,)), ((), ())),
            preferred_element_type=jnp.float32,
        )

    p = product((0, 1), (0, 1), ())
    q = product((0, 2), (2, 0), ((0, 0),))
    r = product((1, 2), (2, 1), ((1, 1), (2, 2)))
    low, high = slice(0, size), slice(size, 2 * size)
    return list(zip(cut, (p[:, low] + q[:, high], p[:, high] + r[:, high], q[:, low] + r[:, low])))


def run(kind, plan, coef, left, right, psi, acc, even, odd):
    pairs, local = left.shape[:2]
    slots = local * pairs
    count = plan[kind, 3 * slots]

    def first(i, halves):
        i = jnp.minimum(i, count - 1)
        p, s, block = [plan[kind, k * slots + i] for k in range(3)]
        for c, half in thirds(left.at[p, s], psi.at[block], False):
            halves[:, c] = (half * coef[s, p]).astype(jnp.bfloat16)

    def second(i, halves):
        p, s = [plan[kind, k * slots + i] for k in range(2)]
        for c, term in thirds(halves, right.at[p, s], True):
            acc[s, :, c] += term

    def two(j, carry):
        i = 2 * j
        first(i + 1, odd)
        second(i, even)
        first(i + 2, even)
        second(i + 1, odd)
        return carry

    @pl.when(count > 0)
    def _():
        first(0, even)
        lax.fori_loop(0, lax.div(count, 2), two, 0)

        @pl.when(lax.rem(count, 2) == 1)
        def _():
            second(count - 1, even)


def plan_kernel(local, source, plan):
    make_plan(source, plan, source.shape[1], local)


def products_kernel(kind, n_opg, plan, coef, left, right, *refs):
    local, sb = left.shape[1:3]
    last = kind == CLASSES - 1
    outs = n_opg if last else 1
    pieces, refs = refs[: -outs - 3 - last], refs[-outs - 3 - last :]
    psi, even, odd = refs[outs : outs + 3]
    acc = refs[-1] if last else refs[0]
    if kind:
        acc[...] = pieces[0][...]
        pieces = pieces[1:]
    else:
        acc[...] = jnp.zeros_like(acc)
    if len(pieces) == 1:
        psi = pieces[0]
    else:
        for i, piece in enumerate(pieces):
            psi[i * local : (i + 1) * local] = piece[...]
    run(kind, plan, coef, left, right, psi, acc, even, odd)
    if last:
        me_opg = lax.axis_index(OPG)
        rows = sb // n_opg
        for r, send in enumerate(refs[:outs]):
            at = pl.multiple_of((r ^ me_opg) * rows, 8)
            send[...] = acc[:, pl.ds(at, rows), :].astype(send.dtype)


SMEM = pl.BlockSpec(memory_space=pltpu.SMEM)
VMEM = pl.BlockSpec(memory_space=pltpu.VMEM)


def products(kind, n_opg, plan, coef, left, right, totals, pieces):
    pairs, local, sb, _ = left.shape
    out_shape = jax.ShapeDtypeStruct((local, sb, sb), jnp.float32)
    scratch = []
    if kind == CLASSES - 1:
        scratch = [pltpu.VMEM(out_shape.shape, out_shape.dtype)]
        out_shape = tuple(
            jax.ShapeDtypeStruct(
                (local, sb // n_opg, sb), jnp.bfloat16 if r % PARTS else jnp.float32
            )
            for r in range(n_opg)
        )
    return pl.pallas_call(
        functools.partial(products_kernel, kind, n_opg),
        out_shape=out_shape,
        in_specs=[SMEM] * 2 + [VMEM] * (2 + len(totals) + len(pieces)),
        out_specs=jax.tree.map(lambda _: VMEM, out_shape),
        scratch_shapes=[
            pltpu.VMEM((len(pieces) * local, sb, sb), jnp.bfloat16),
            pltpu.VMEM((sb, sb), jnp.bfloat16),
            pltpu.VMEM((sb, sb), jnp.bfloat16),
            *scratch,
        ],
        compiler_params=pltpu.CompilerParams(vmem_limit_bytes=KERNEL_VMEM),
        cost_estimate=pl.CostEstimate(flops=sb, bytes_accessed=0, transcendentals=0),
    )(plan, coef, left, right, *totals, *pieces)


def scatter_sum(sends, n_opg):
    out = []
    for high in reversed(range(n_opg // PARTS)):
        at = high * PARTS
        total = sends[at]
        for low in (3, 1, 2):
            total = total + flip(sends[at + low], OPG, n_opg, low).astype(jnp.float32)
        if high:
            total = flip(total.astype(jnp.bfloat16), OPG, n_opg, at).astype(jnp.float32)
        out.append(total)
    return sum(out[:-1], out[-1])


def on_device(n_opg, n_sec, psi, left_ops, right_ops, source, coef_index, sixj):
    local, sb, _ = psi.shape
    pairs = left_ops.shape[0]

    half = lax.rem(lax.axis_index(OPG), HALVES)
    cut = psi[local - 1].reshape(HALVES, sb // HALVES, sb)
    ours = lax.dynamic_index_in_dim(cut, half, axis=0, keepdims=False)
    ours, rest, psi = lax.optimization_barrier((ours, psi[: local - 1], psi))
    here, whole = {0: ours}, {0: rest}
    for bit in bits_of(n_sec)[1:]:
        for held in (here, whole):
            held.update({r | bit: flip(x, SEC, n_sec, bit) for r, x in held.items()})
    far = range(NEAR, n_sec, 2)
    here, whole = [here[r] for r in far], [whole[r] for r in far]
    partner = flip(psi, SEC, n_sec, 1)

    plan = pl.pallas_call(
        functools.partial(plan_kernel, local),
        out_shape=jax.ShapeDtypeStruct((CLASSES, 3 * local * pairs + 1), jnp.int32),
        in_specs=[SMEM],
        out_specs=SMEM,
        compiler_params=pltpu.CompilerParams(vmem_limit_bytes=KERNEL_VMEM),
        cost_estimate=pl.CostEstimate(flops=PLAN_FLOPS, bytes_accessed=0, transcendentals=0),
    )(source.T)
    plan, coef_index = lax.optimization_barrier((plan, coef_index))
    table = jnp.arange(sixj.shape[0], dtype=jnp.int32)
    coef = jnp.sum(jnp.where(coef_index.T[:, :, None] == table, sixj, 0.0), axis=2)

    def onto(kind, totals, pieces):
        return products(kind, n_opg, plan, coef, left_ops, right_ops, totals, pieces)

    def to_other_core(pieces):
        return [flip(x, SEC, n_sec, 1) for x in pieces]

    here, plan, coef = lax.optimization_barrier((here, plan, coef))
    there = [flip(x, OPG, n_opg, 1) for x in here]
    done = onto(0, [], [psi, partner])
    here, there, whole, done = lax.optimization_barrier((here, there, whole, done))
    twins = []
    for one, other, rest in zip(here, there, whole):
        upper, lower = jnp.where(half == 0, one, other), jnp.where(half == 0, other, one)
        rows = jnp.concatenate([rest.reshape(-1, sb), upper, lower])
        twins.append(rows.reshape(local, sb, sb))
    others = to_other_core(twins)
    done = onto(1, [done], twins)
    sends = onto(2, [done], others)
    return jnp.swapaxes(scatter_sum(sends, n_opg), 0, 1).astype(jnp.bfloat16)


def solution(mesh):
    n_opg, n_sec = mesh.shape[OPG], mesh.shape[SEC]
    placed = (
        P(SEC, None, None),
        P(OPG, SEC, None, None),
        P(OPG, SEC, None, None),
        P(OPG, SEC),
        P(OPG, SEC),
        P(),
    )
    return jax.shard_map(
        functools.partial(on_device, n_opg, n_sec),
        mesh=mesh,
        in_specs=placed,
        out_specs=P(OPG, SEC, None),
        check_vma=False,
    )
```

```python
import functools

import jax
import jax.numpy as jnp
from jax import lax
from jax.experimental import pallas as pl
from jax.experimental.pallas import tpu as pltpu
from jax.sharding import PartitionSpec as P

OPG = "opg"
SEC = "sec"
PARTS = 4
HALVES = 2
NEAR = 2
KERNEL_VMEM = 24_000_000
PLAN_FLOPS = 20_000_000_000
PLAN_VMEM = 49_000_000
NEAR_VMEM = 44_000_000


def flip(x, axis, size, bit):
    return lax.ppermute(x, axis, [(i, i ^ bit) for i in range(size)])


def bits_of(size):
    return [1 << k for k in range(size.bit_length() - 1)]


CLASSES = 3


def make_plan(source, plan, pairs, local):
    slots = local * pairs
    for kind in range(CLASSES):
        plan[kind, 3 * slots] = 0
    me_sec = lax.axis_index(SEC)

    def sector(s):
        def one(p, carry):
            src = source[s, p]
            r, j = lax.div(src, local) ^ me_sec, lax.rem(src, local)
            kind = jnp.where(r < NEAR, 0, 1 + lax.rem(r, 2))
            block = jnp.where(r < NEAR, r, lax.div(r, 2) - 1) * local + j
            n = plan[kind, 3 * slots]
            plan[kind, n] = p
            plan[kind, slots + n] = s
            plan[kind, 2 * slots + n] = block
            plan[kind, 3 * slots] = n + 1
            return carry

        lax.fori_loop(0, pairs, one, 0)

    for s in range(local):
        sector(s)


def thirds(x, w, transposed):
    size = x.shape[1] // 3
    cut = [slice(i * size, (i + 1) * size) for i in range(3)]
    none = jnp.zeros((size, size), w.dtype)

    def tile(depth, columns, absent):
        def block(k, n):
            if (k, n) in absent:
                return none
            return w[cut[n], cut[k]] if transposed else w[cut[k], cut[n]]

        one, two = (columns, depth) if transposed else (depth, columns)
        rows = [
            jnp.concatenate(
                [block(j, i) if transposed else block(i, j) for j in two], axis=1
            )
            for i in one
        ]
        return jnp.concatenate(rows, axis=0)

    def product(depth, columns, absent):
        return lax.dot_general(
            jnp.concatenate([x[:, cut[k]] for k in depth], axis=1),
            tile(depth, columns, absent),
            (((1,), (1 if transposed else 0,)), ((), ())),
            preferred_element_type=jnp.float32,
        )

    p = product((0, 1), (0, 1), ())
    q = product((0, 2), (2, 0), ((0, 0),))
    r = product((1, 2), (2, 1), ((1, 1), (2, 2)))
    low, high = slice(0, size), slice(size, 2 * size)
    return list(zip(cut, (p[:, low] + q[:, high], p[:, high] + r[:, high], q[:, low] + r[:, low])))


def run(kind, plan, coef, left, right, psi, acc, even, odd, ready):
    pairs, local = left.shape[:2]
    slots = local * pairs
    count = plan[kind, 3 * slots]

    def first(i, halves):
        i = jnp.minimum(i, count - 1)
        p, s, block = [plan[kind, k * slots + i] for k in range(3)]
        for c, half in thirds(left.at[p, s], psi.at[block], False):
            halves[:, c] = (half * coef[s, p]).astype(jnp.bfloat16)

    def second(i, halves):
        p, s = [plan[kind, k * slots + i] for k in range(2)]
        for c, term in thirds(halves, right.at[p, s], True):
            acc[s, :, c] += term

    def two(j, carry):
        i = 2 * j
        ready(i)
        ready(i + 1)
        first(i + 1, odd)
        second(i, even)
        first(i + 2, even)
        second(i + 1, odd)
        return carry

    @pl.when(count > 0)
    def _():
        first(0, even)
        lax.fori_loop(0, lax.div(count, 2), two, 0)

        @pl.when(lax.rem(count, 2) == 1)
        def _():
            ready(count - 1)
            second(count - 1, even)


def plan_kernel(source, left, plan, left_here, sem):
    pairs, local = left.shape[:2]
    copies = [
        pltpu.make_async_copy(left.at[p], left_here.at[p], sem.at[p]) for p in range(pairs)
    ]
    for copy in copies:
        copy.start()
    make_plan(source, plan, pairs, local)
    for copy in copies:
        copy.wait()


def near_kernel(plan, coef, left, right, own, partner, acc, right_here, psi, even, odd, sem):
    pairs, local = right.shape[:2]
    slots = pairs * local

    def copy(kind, i):
        p, s = plan[kind, i], plan[kind, slots + i]
        return pltpu.make_async_copy(
            right.at[p, s], right_here.at[p, s], sem.at[p * local + s]
        )

    def each(kind, act):
        def one(i, carry):
            act(kind, i)
            return carry

        lax.fori_loop(0, plan[kind, 3 * slots], one, 0)

    for kind in range(CLASSES):
        each(kind, lambda kind, i: copy(kind, i).start())
    acc[...] = jnp.zeros_like(acc)
    psi[:local] = own[...]
    psi[local:] = partner[...]
    run(
        0, plan, coef, left, right_here, psi, acc, even, odd, lambda i: copy(0, i).wait()
    )
    for kind in range(1, CLASSES):
        each(kind, lambda kind, i: copy(kind, i).wait())


def products_kernel(kind, n_opg, plan, coef, left, right, total, *refs):
    local, sb = left.shape[1:3]
    last = kind == CLASSES - 1
    outs = n_opg if last else 1
    pieces, refs = refs[: -outs - 3 - last], refs[-outs - 3 - last :]
    psi, even, odd = refs[outs : outs + 3]
    acc = refs[-1] if last else refs[0]
    acc[...] = total[...]
    if len(pieces) == 1:
        psi = pieces[0]
    else:
        for i, piece in enumerate(pieces):
            psi[i * local : (i + 1) * local] = piece[...]
    run(kind, plan, coef, left, right, psi, acc, even, odd, lambda i: None)
    if last:
        me_opg = lax.axis_index(OPG)
        rows = sb // n_opg
        for r, send in enumerate(refs[:outs]):
            at = pl.multiple_of((r ^ me_opg) * rows, 8)
            send[...] = acc[:, pl.ds(at, rows), :].astype(send.dtype)


SMEM = pl.BlockSpec(memory_space=pltpu.SMEM)
VMEM = pl.BlockSpec(memory_space=pltpu.VMEM)
HBM = pl.BlockSpec(memory_space=pltpu.HBM)


def halves(sb):
    return [pltpu.VMEM((sb, sb), jnp.bfloat16), pltpu.VMEM((sb, sb), jnp.bfloat16)]


def lists(source, left):
    pairs, local = left.shape[:2]
    return pl.pallas_call(
        plan_kernel,
        out_shape=(
            jax.ShapeDtypeStruct((CLASSES, 3 * local * pairs + 1), jnp.int32),
            jax.ShapeDtypeStruct(left.shape, left.dtype),
        ),
        in_specs=[SMEM, HBM],
        out_specs=(SMEM, VMEM),
        scratch_shapes=[pltpu.SemaphoreType.DMA((pairs,))],
        compiler_params=pltpu.CompilerParams(vmem_limit_bytes=PLAN_VMEM),
        cost_estimate=pl.CostEstimate(flops=PLAN_FLOPS, bytes_accessed=0, transcendentals=0),
    )(source, left)


def near_products(plan, coef, left, right, own, partner):
    pairs, local, sb, _ = right.shape
    return pl.pallas_call(
        near_kernel,
        out_shape=(
            jax.ShapeDtypeStruct((local, sb, sb), jnp.float32),
            jax.ShapeDtypeStruct(right.shape, right.dtype),
        ),
        in_specs=[SMEM, SMEM, VMEM, HBM, VMEM, VMEM],
        out_specs=(VMEM, VMEM),
        scratch_shapes=[
            pltpu.VMEM((NEAR * local, sb, sb), jnp.bfloat16),
            *halves(sb),
            pltpu.SemaphoreType.DMA((pairs * local,)),
        ],
        compiler_params=pltpu.CompilerParams(vmem_limit_bytes=NEAR_VMEM),
        cost_estimate=pl.CostEstimate(flops=sb, bytes_accessed=0, transcendentals=0),
    )(plan, coef, left, right, own, partner)


def products(kind, n_opg, plan, coef, left, right, total, pieces):
    pairs, local, sb, _ = left.shape
    out_shape = jax.ShapeDtypeStruct(total.shape, total.dtype)
    scratch = []
    if kind == CLASSES - 1:
        scratch = [pltpu.VMEM(out_shape.shape, out_shape.dtype)]
        out_shape = tuple(
            jax.ShapeDtypeStruct(
                (local, sb // n_opg, sb), jnp.bfloat16 if r % PARTS else jnp.float32
            )
            for r in range(n_opg)
        )
    return pl.pallas_call(
        functools.partial(products_kernel, kind, n_opg),
        out_shape=out_shape,
        in_specs=[SMEM] * 2 + [VMEM] * (3 + len(pieces)),
        out_specs=jax.tree.map(lambda _: VMEM, out_shape),
        scratch_shapes=[
            pltpu.VMEM((len(pieces) * local, sb, sb), jnp.bfloat16),
            *halves(sb),
            *scratch,
        ],
        compiler_params=pltpu.CompilerParams(vmem_limit_bytes=KERNEL_VMEM),
        cost_estimate=pl.CostEstimate(flops=sb, bytes_accessed=0, transcendentals=0),
    )(plan, coef, left, right, total, *pieces)


def scatter_sum(sends, n_opg):
    out = []
    for high in reversed(range(n_opg // PARTS)):
        at = high * PARTS
        total = sends[at]
        for low in (3, 1, 2):
            total = total + flip(sends[at + low], OPG, n_opg, low).astype(jnp.float32)
        if high:
            total = flip(total.astype(jnp.bfloat16), OPG, n_opg, at).astype(jnp.float32)
        out.append(total)
    return sum(out[:-1], out[-1])


def on_device(n_opg, n_sec, psi, left_ops, right_ops, source, coef_index, sixj):
    local, sb, _ = psi.shape

    half = lax.rem(lax.axis_index(OPG), HALVES)
    cut = psi[local - 1].reshape(HALVES, sb // HALVES, sb)
    ours = lax.dynamic_index_in_dim(cut, half, axis=0, keepdims=False)
    ours, rest, psi = lax.optimization_barrier((ours, psi[: local - 1], psi))
    here, whole = {0: ours}, {0: rest}
    for bit in bits_of(n_sec)[1:]:
        for held in (here, whole):
            held.update({r | bit: flip(x, SEC, n_sec, bit) for r, x in held.items()})
    far = range(NEAR, n_sec, 2)
    here, whole = [here[r] for r in far], [whole[r] for r in far]
    partner = flip(psi, SEC, n_sec, 1)

    plan, left = lists(source.T, left_ops)
    plan, left, coef_index = lax.optimization_barrier((plan, left, coef_index))
    table = jnp.arange(sixj.shape[0], dtype=jnp.int32)
    coef = jnp.sum(jnp.where(coef_index.T[:, :, None] == table, sixj, 0.0), axis=2)

    def to_other_core(pieces):
        return [flip(x, SEC, n_sec, 1) for x in pieces]

    here, plan, coef = lax.optimization_barrier((here, plan, coef))
    there = [flip(x, OPG, n_opg, 1) for x in here]
    done, right = near_products(plan, coef, left, right_ops, psi, partner)
    here, there, whole, done = lax.optimization_barrier((here, there, whole, done))
    twins = []
    for one, other, rest in zip(here, there, whole):
        upper, lower = jnp.where(half == 0, one, other), jnp.where(half == 0, other, one)
        rows = jnp.concatenate([rest.reshape(-1, sb), upper, lower])
        twins.append(rows.reshape(local, sb, sb))
    others = to_other_core(twins)
    done = products(1, n_opg, plan, coef, left, right, done, twins)
    sends = products(2, n_opg, plan, coef, left, right, done, others)
    return jnp.swapaxes(scatter_sum(sends, n_opg), 0, 1).astype(jnp.bfloat16)


def solution(mesh):
    n_opg, n_sec = mesh.shape[OPG], mesh.shape[SEC]
    placed = (
        P(SEC, None, None),
        P(OPG, SEC, None, None),
        P(OPG, SEC, None, None),
        P(OPG, SEC),
        P(OPG, SEC),
        P(),
    )
    return jax.shard_map(
        functools.partial(on_device, n_opg, n_sec),
        mesh=mesh,
        in_specs=placed,
        out_specs=P(OPG, SEC, None),
        check_vma=False,
    )
```

```python
import functools

import jax
import jax.numpy as jnp
from jax import lax
from jax.experimental import pallas as pl
from jax.experimental.pallas import tpu as pltpu
from jax.sharding import PartitionSpec as P

OPG = "opg"
SEC = "sec"
PARTS = 4
HALVES = 2
NEAR = 2
KERNEL_VMEM = 24_000_000
PLAN_FLOPS = 200_000_000_000


def flip(x, axis, size, bit):
    return lax.ppermute(x, axis, [(i, i ^ bit) for i in range(size)])


def bits_of(size):
    return [1 << k for k in range(size.bit_length() - 1)]


CLASSES = 3


def make_plan(meta, plan, scale, pairs, local):
    slots = local * pairs
    for kind in range(CLASSES):
        plan[kind, 3 * slots] = 0
    me_sec = lax.axis_index(SEC)

    def sector(s):
        def one(p, carry):
            src = meta[s, p].astype(jnp.int32)
            r, j = lax.div(src, local) ^ me_sec, lax.rem(src, local)
            kind = jnp.where(r < NEAR, 0, 1 + lax.rem(r, 2))
            block = jnp.where(r < NEAR, r, lax.div(r, 2) - 1) * local + j
            n = plan[kind, 3 * slots]
            plan[kind, n] = p
            plan[kind, slots + n] = s
            plan[kind, 2 * slots + n] = block
            scale[kind, n] = meta[local + s, p]
            plan[kind, 3 * slots] = n + 1
            return carry

        lax.fori_loop(0, pairs, one, 0)

    for s in range(local):
        sector(s)


def thirds(x, w, transposed):
    size = x.shape[1] // 3
    cut = [slice(i * size, (i + 1) * size) for i in range(3)]
    none = jnp.zeros((size, size), w.dtype)

    def tile(depth, columns, absent):
        def block(k, n):
            if (k, n) in absent:
                return none
            return w[cut[n], cut[k]] if transposed else w[cut[k], cut[n]]

        one, two = (columns, depth) if transposed else (depth, columns)
        rows = [
            jnp.concatenate(
                [block(j, i) if transposed else block(i, j) for j in two], axis=1
            )
            for i in one
        ]
        return jnp.concatenate(rows, axis=0)

    def product(depth, columns, absent):
        return lax.dot_general(
            jnp.concatenate([x[:, cut[k]] for k in depth], axis=1),
            tile(depth, columns, absent),
            (((1,), (1 if transposed else 0,)), ((), ())),
            preferred_element_type=jnp.float32,
        )

    p = product((0, 1), (0, 1), ())
    q = product((0, 2), (2, 0), ((0, 0),))
    r = product((1, 2), (2, 1), ((1, 1), (2, 2)))
    low, high = slice(0, size), slice(size, 2 * size)
    return list(zip(cut, (p[:, low] + q[:, high], p[:, high] + r[:, high], q[:, low] + r[:, low])))


def run(kind, plan, scale, left, right, psi, acc, even, odd):
    pairs, local = left.shape[:2]
    slots = local * pairs
    count = plan[kind, 3 * slots]

    def first(i, halves):
        i = jnp.minimum(i, count - 1)
        p, s, block = [plan[kind, k * slots + i] for k in range(3)]
        for c, half in thirds(left.at[p, s], psi.at[block], False):
            halves[:, c] = (half * scale[kind, i]).astype(jnp.bfloat16)

    def second(i, halves):
        p, s = [plan[kind, k * slots + i] for k in range(2)]
        for c, term in thirds(halves, right.at[p, s], True):
            acc[s, :, c] += term

    def two(j, carry):
        i = 2 * j
        first(i + 1, odd)
        second(i, even)
        first(i + 2, even)
        second(i + 1, odd)
        return carry

    @pl.when(count > 0)
    def _():
        first(0, even)
        lax.fori_loop(0, lax.div(count, 2), two, 0)

        @pl.when(lax.rem(count, 2) == 1)
        def _():
            second(count - 1, even)


def plan_kernel(local, meta, plan, scale):
    make_plan(meta, plan, scale, meta.shape[1], local)


def products_kernel(kind, n_opg, plan, scale, left, right, *refs):
    local, sb = left.shape[1:3]
    last = kind == CLASSES - 1
    outs = n_opg if last else 1
    pieces, refs = refs[: -outs - 3 - last], refs[-outs - 3 - last :]
    psi, even, odd = refs[outs : outs + 3]
    acc = refs[-1] if last else refs[0]
    if kind:
        acc[...] = pieces[0][...]
        pieces = pieces[1:]
    else:
        acc[...] = jnp.zeros_like(acc)
    if kind == 0:
        for i, piece in enumerate(pieces):
            psi[i * local : (i + 1) * local] = piece[...]
    else:
        half = lax.rem(lax.axis_index(OPG), HALVES)
        rows = sb // HALVES
        for i in range(len(pieces) // 2):
            whole, halves = pieces[2 * i : 2 * i + 2]
            end = (i + 1) * local - 1
            psi[i * local : end] = whole[...]
            psi[end, pl.ds(pl.multiple_of(half * rows, 16), rows), :] = halves[0]
            psi[end, pl.ds(pl.multiple_of((1 - half) * rows, 16), rows), :] = halves[1]
    run(kind, plan, scale, left, right, psi, acc, even, odd)
    if last:
        me_opg = lax.axis_index(OPG)
        rows = sb // n_opg
        for r, send in enumerate(refs[:outs]):
            at = pl.multiple_of((r ^ me_opg) * rows, 8)
            send[...] = acc[:, pl.ds(at, rows), :].astype(send.dtype)


SMEM = pl.BlockSpec(memory_space=pltpu.SMEM)
VMEM = pl.BlockSpec(memory_space=pltpu.VMEM)


def products(kind, n_opg, plan, scale, left, right, totals, pieces):
    pairs, local, sb, _ = left.shape
    out_shape = jax.ShapeDtypeStruct((local, sb, sb), jnp.float32)
    scratch = []
    if kind == CLASSES - 1:
        scratch = [pltpu.VMEM(out_shape.shape, out_shape.dtype)]
        out_shape = tuple(
            jax.ShapeDtypeStruct(
                (local, sb // n_opg, sb), jnp.bfloat16 if r % PARTS else jnp.float32
            )
            for r in range(n_opg)
        )
    return pl.pallas_call(
        functools.partial(products_kernel, kind, n_opg),
        out_shape=out_shape,
        in_specs=[SMEM] * 2 + [VMEM] * (2 + len(totals) + len(pieces)),
        out_specs=jax.tree.map(lambda _: VMEM, out_shape),
        scratch_shapes=[
            pltpu.VMEM((len(pieces) // (2 if kind else 1) * local, sb, sb), jnp.bfloat16),
            pltpu.VMEM((sb, sb), jnp.bfloat16),
            pltpu.VMEM((sb, sb), jnp.bfloat16),
            *scratch,
        ],
        compiler_params=pltpu.CompilerParams(vmem_limit_bytes=KERNEL_VMEM),
        cost_estimate=pl.CostEstimate(flops=sb, bytes_accessed=0, transcendentals=0),
    )(plan, scale, left, right, *totals, *pieces)


def scatter_sum(sends, n_opg):
    out = []
    for high in reversed(range(n_opg // PARTS)):
        at = high * PARTS
        total = sends[at]
        for low in (3, 1, 2):
            total = total + flip(sends[at + low], OPG, n_opg, low).astype(jnp.float32)
        if high:
            total = flip(total.astype(jnp.bfloat16), OPG, n_opg, at).astype(jnp.float32)
        out.append(total)
    return sum(out[:-1], out[-1])


def on_device(n_opg, n_sec, psi, left_ops, right_ops, source, coef_index, sixj):
    local, sb, _ = psi.shape
    pairs = left_ops.shape[0]

    half = lax.rem(lax.axis_index(OPG), HALVES)
    cut = psi[local - 1].reshape(HALVES, sb // HALVES, sb)
    ours = lax.dynamic_index_in_dim(cut, half, axis=0, keepdims=False)
    ours, rest, psi = lax.optimization_barrier((ours, psi[: local - 1], psi))
    here, whole = {0: ours}, {0: rest}
    for bit in bits_of(n_sec)[1:]:
        for held in (here, whole):
            held.update({r | bit: flip(x, SEC, n_sec, bit) for r, x in held.items()})
    far = range(NEAR, n_sec, 2)
    here, whole = [here[r] for r in far], [whole[r] for r in far]
    partner = flip(psi, SEC, n_sec, 1)

    table = jnp.arange(sixj.shape[0], dtype=jnp.int32)
    coef = jnp.sum(jnp.where(coef_index.T[:, :, None] == table, sixj, 0.0), axis=2)
    meta = jnp.concatenate([source.T.astype(jnp.float32), coef])
    plan, scale = pl.pallas_call(
        functools.partial(plan_kernel, local),
        out_shape=(
            jax.ShapeDtypeStruct((CLASSES, 3 * local * pairs + 1), jnp.int32),
            jax.ShapeDtypeStruct((CLASSES, local * pairs), jnp.float32),
        ),
        in_specs=[SMEM],
        out_specs=(SMEM, SMEM),
        compiler_params=pltpu.CompilerParams(vmem_limit_bytes=KERNEL_VMEM),
        cost_estimate=pl.CostEstimate(flops=PLAN_FLOPS, bytes_accessed=0, transcendentals=0),
    )(meta)

    def onto(kind, totals, pieces):
        return products(kind, n_opg, plan, scale, left_ops, right_ops, totals, pieces)

    def to_other_core(pieces):
        return [flip(x, SEC, n_sec, 1) for x in pieces]

    here, plan, scale = lax.optimization_barrier((here, plan, scale))
    there = [flip(x, OPG, n_opg, 1) for x in here]
    done = onto(0, [], [psi, partner])
    here, there, whole, done = lax.optimization_barrier((here, there, whole, done))
    whole_crossed = to_other_core(whole)
    halves = [jnp.stack(two) for two in zip(here, there)]
    halves_crossed = to_other_core(halves)
    done = onto(1, [done], [x for two in zip(whole, halves) for x in two])
    sends = onto(2, [done], [x for two in zip(whole_crossed, halves_crossed) for x in two])
    return jnp.swapaxes(scatter_sum(sends, n_opg), 0, 1).astype(jnp.bfloat16)


def solution(mesh):
    n_opg, n_sec = mesh.shape[OPG], mesh.shape[SEC]
    placed = (
        P(SEC, None, None),
        P(OPG, SEC, None, None),
        P(OPG, SEC, None, None),
        P(OPG, SEC),
        P(OPG, SEC),
        P(),
    )
    return jax.shard_map(
        functools.partial(on_device, n_opg, n_sec),
        mesh=mesh,
        in_specs=placed,
        out_specs=P(OPG, SEC, None),
        check_vma=False,
    )
```

```python
import functools

import jax
import jax.numpy as jnp
from jax import lax
from jax.experimental import pallas as pl
from jax.experimental.pallas import tpu as pltpu
from jax.sharding import PartitionSpec as P

OPG = "opg"
SEC = "sec"
PARTS = 4
HALVES = 2
NEAR = 2
KERNEL_VMEM = 24_000_000
PLAN_FLOPS = 5_000_000_000


def flip(x, axis, size, bit):
    return lax.ppermute(x, axis, [(i, i ^ bit) for i in range(size)])


def bits_of(size):
    return [1 << k for k in range(size.bit_length() - 1)]


CLASSES = 3


def make_plan(source, plan, pairs, local):
    slots = local * pairs
    for kind in range(CLASSES):
        plan[kind, 3 * slots] = 0
    me_sec = lax.axis_index(SEC)

    def sector(s):
        def one(p, carry):
            src = source[s, p]
            r, j = lax.div(src, local) ^ me_sec, lax.rem(src, local)
            kind = jnp.where(r < NEAR, 0, 1 + lax.rem(r, 2))
            block = jnp.where(r < NEAR, r, lax.div(r, 2) - 1) * local + j
            n = plan[kind, 3 * slots]
            plan[kind, n] = p
            plan[kind, slots + n] = s
            plan[kind, 2 * slots + n] = block
            plan[kind, 3 * slots] = n + 1
            return carry

        lax.fori_loop(0, pairs, one, 0)

    for s in range(local):
        sector(s)


def thirds(x, w, transposed):
    size = x.shape[1] // 3
    cut = [slice(i * size, (i + 1) * size) for i in range(3)]
    none = jnp.zeros((size, size), w.dtype)

    def tile(depth, columns, absent):
        def block(k, n):
            if (k, n) in absent:
                return none
            return w[cut[n], cut[k]] if transposed else w[cut[k], cut[n]]

        one, two = (columns, depth) if transposed else (depth, columns)
        rows = [
            jnp.concatenate(
                [block(j, i) if transposed else block(i, j) for j in two], axis=1
            )
            for i in one
        ]
        return jnp.concatenate(rows, axis=0)

    def product(depth, columns, absent):
        return lax.dot_general(
            jnp.concatenate([x[:, cut[k]] for k in depth], axis=1),
            tile(depth, columns, absent),
            (((1,), (1 if transposed else 0,)), ((), ())),
            preferred_element_type=jnp.float32,
        )

    p = product((0, 1), (0, 1), ())
    q = product((0, 2), (2, 0), ((0, 0),))
    r = product((1, 2), (2, 1), ((1, 1), (2, 2)))
    low, high = slice(0, size), slice(size, 2 * size)
    return list(zip(cut, (p[:, low] + q[:, high], p[:, high] + r[:, high], q[:, low] + r[:, low])))


def run(kind, plan, coef, left, right, psi, acc, even, odd):
    pairs, local = left.shape[:2]
    slots = local * pairs
    count = plan[kind, 3 * slots]

    def first(i, halves):
        i = jnp.minimum(i, count - 1)
        p, s, block = [plan[kind, k * slots + i] for k in range(3)]
        for c, half in thirds(left.at[p, s], psi.at[block], False):
            halves[:, c] = (half * coef[s, p]).astype(jnp.bfloat16)

    def second(i, halves):
        p, s = [plan[kind, k * slots + i] for k in range(2)]
        for c, term in thirds(halves, right.at[p, s], True):
            acc[s, :, c] += term

    def two(j, carry):
        i = 2 * j
        first(i + 1, odd)
        second(i, even)
        first(i + 2, even)
        second(i + 1, odd)
        return carry

    @pl.when(count > 0)
    def _():
        first(0, even)
        lax.fori_loop(0, lax.div(count, 2), two, 0)

        @pl.when(lax.rem(count, 2) == 1)
        def _():
            second(count - 1, even)


def plan_kernel(local, source, plan):
    make_plan(source, plan, source.shape[1], local)


def products_kernel(kind, n_opg, plan, coef, left, right, *refs):
    local, sb = left.shape[1:3]
    last = kind == CLASSES - 1
    outs = n_opg if last else 1
    pieces, refs = refs[: -outs - 3 - last], refs[-outs - 3 - last :]
    psi, even, odd = refs[outs : outs + 3]
    acc = refs[-1] if last else refs[0]
    if kind:
        acc[...] = pieces[0][...]
        pieces = pieces[1:]
    else:
        acc[...] = jnp.zeros_like(acc)
    if len(pieces) == 1:
        psi = pieces[0]
    else:
        for i, piece in enumerate(pieces):
            psi[i * local : (i + 1) * local] = piece[...]
    run(kind, plan, coef, left, right, psi, acc, even, odd)
    if last:
        me_opg = lax.axis_index(OPG)
        rows = sb // n_opg
        for r, send in enumerate(refs[:outs]):
            at = pl.multiple_of((r ^ me_opg) * rows, 8)
            send[...] = acc[:, pl.ds(at, rows), :].astype(send.dtype)


SMEM = pl.BlockSpec(memory_space=pltpu.SMEM)
VMEM = pl.BlockSpec(memory_space=pltpu.VMEM)


def products(kind, n_opg, plan, coef, left, right, totals, pieces):
    pairs, local, sb, _ = left.shape
    out_shape = jax.ShapeDtypeStruct((local, sb, sb), jnp.float32)
    scratch = []
    if kind == CLASSES - 1:
        scratch = [pltpu.VMEM(out_shape.shape, out_shape.dtype)]
        out_shape = tuple(
            jax.ShapeDtypeStruct(
                (local, sb // n_opg, sb), jnp.bfloat16 if r % PARTS else jnp.float32
            )
            for r in range(n_opg)
        )
    return pl.pallas_call(
        functools.partial(products_kernel, kind, n_opg),
        out_shape=out_shape,
        in_specs=[SMEM] * 2 + [VMEM] * (2 + len(totals) + len(pieces)),
        out_specs=jax.tree.map(lambda _: VMEM, out_shape),
        scratch_shapes=[
            pltpu.VMEM((len(pieces) * local, sb, sb), jnp.bfloat16),
            pltpu.VMEM((sb, sb), jnp.bfloat16),
            pltpu.VMEM((sb, sb), jnp.bfloat16),
            *scratch,
        ],
        compiler_params=pltpu.CompilerParams(vmem_limit_bytes=KERNEL_VMEM),
        cost_estimate=pl.CostEstimate(flops=sb, bytes_accessed=0, transcendentals=0),
    )(plan, coef, left, right, *totals, *pieces)


def scatter_sum(sends, n_opg):
    out = []
    for high in reversed(range(n_opg // PARTS)):
        at = high * PARTS
        total = sends[at]
        for low in (3, 1, 2):
            total = total + flip(sends[at + low], OPG, n_opg, low).astype(jnp.float32)
        if high:
            total = flip(total.astype(jnp.bfloat16), OPG, n_opg, at).astype(jnp.float32)
        out.append(total)
    return sum(out[:-1], out[-1])


def on_device(n_opg, n_sec, psi, left_ops, right_ops, source, coef_index, sixj):
    local, sb, _ = psi.shape
    pairs = left_ops.shape[0]

    half = lax.rem(lax.axis_index(OPG), HALVES)
    cut = psi[local - 1].reshape(HALVES, sb // HALVES, sb)
    ours = lax.dynamic_index_in_dim(cut, half, axis=0, keepdims=False)
    ours, rest, psi = lax.optimization_barrier((ours, psi[: local - 1], psi))
    here, whole = {0: ours}, {0: rest}
    for bit in bits_of(n_sec)[1:]:
        for held in (here, whole):
            held.update({r | bit: flip(x, SEC, n_sec, bit) for r, x in held.items()})
    far = range(NEAR, n_sec, 2)
    here, whole = [here[r] for r in far], [whole[r] for r in far]
    partner = flip(psi, SEC, n_sec, 1)

    plan = pl.pallas_call(
        functools.partial(plan_kernel, local),
        out_shape=jax.ShapeDtypeStruct((CLASSES, 3 * local * pairs + 1), jnp.int32),
        in_specs=[SMEM],
        out_specs=SMEM,
        compiler_params=pltpu.CompilerParams(vmem_limit_bytes=KERNEL_VMEM),
        cost_estimate=pl.CostEstimate(flops=PLAN_FLOPS, bytes_accessed=0, transcendentals=0),
    )(source.T)
    plan, coef_index = lax.optimization_barrier((plan, coef_index))
    table = jnp.arange(sixj.shape[0], dtype=jnp.int32)
    coef = jnp.sum(jnp.where(coef_index.T[:, :, None] == table, sixj, 0.0), axis=2)

    def onto(kind, totals, pieces):
        return products(kind, n_opg, plan, coef, left_ops, right_ops, totals, pieces)

    def to_other_core(pieces):
        return [flip(x, SEC, n_sec, 1) for x in pieces]

    here, plan, coef = lax.optimization_barrier((here, plan, coef))
    there = [flip(x, OPG, n_opg, 1) for x in here]
    done = onto(0, [], [psi, partner])
    here, there, whole, done = lax.optimization_barrier((here, there, whole, done))
    twins = []
    for one, other, rest in zip(here, there, whole):
        upper, lower = jnp.where(half == 0, one, other), jnp.where(half == 0, other, one)
        rows = jnp.concatenate([rest.reshape(-1, sb), upper, lower])
        twins.append(rows.reshape(local, sb, sb))
    others = to_other_core(twins)
    done = onto(1, [done], twins)
    sends = onto(2, [done], others)
    return jnp.swapaxes(scatter_sum(sends, n_opg), 0, 1).astype(jnp.bfloat16)


def solution(mesh):
    n_opg, n_sec = mesh.shape[OPG], mesh.shape[SEC]
    placed = (
        P(SEC, None, None),
        P(OPG, SEC, None, None),
        P(OPG, SEC, None, None),
        P(OPG, SEC),
        P(OPG, SEC),
        P(),
    )
    return jax.shard_map(
        functools.partial(on_device, n_opg, n_sec),
        mesh=mesh,
        in_specs=placed,
        out_specs=P(OPG, SEC, None),
        check_vma=False,
    )
```

```python
import functools

import jax
import jax.numpy as jnp
from jax import lax
from jax.experimental import pallas as pl
from jax.experimental.pallas import tpu as pltpu
from jax.sharding import PartitionSpec as P

OPG = "opg"
SEC = "sec"
PARTS = 4
HALVES = 2
NEAR = 2
KERNEL_VMEM = 24_000_000
PLAN_FLOPS = 20_000_000_000


def flip(x, axis, size, bit):
    return lax.ppermute(x, axis, [(i, i ^ bit) for i in range(size)])


def bits_of(size):
    return [1 << k for k in range(size.bit_length() - 1)]


CLASSES = 3


def make_plan(source, plan, pairs, local):
    slots = local * pairs
    for kind in range(CLASSES):
        plan[kind, 3 * slots] = 0
    me_sec = lax.axis_index(SEC)

    def sector(s):
        def one(p, carry):
            src = source[s, p]
            r, j = lax.div(src, local) ^ me_sec, lax.rem(src, local)
            kind = jnp.where(r < NEAR, 0, 1 + lax.rem(r, 2))
            block = jnp.where(r < NEAR, r, lax.div(r, 2) - 1) * local + j
            n = plan[kind, 3 * slots]
            plan[kind, n] = p
            plan[kind, slots + n] = s
            plan[kind, 2 * slots + n] = block
            plan[kind, 3 * slots] = n + 1
            return carry

        lax.fori_loop(0, pairs, one, 0)

    for s in range(local):
        sector(s)


def thirds(x, w, transposed):
    size = x.shape[1] // 3
    cut = [slice(i * size, (i + 1) * size) for i in range(3)]
    none = jnp.zeros((size, size), w.dtype)

    def tile(depth, columns, absent):
        def block(k, n):
            if (k, n) in absent:
                return none
            return w[cut[n], cut[k]] if transposed else w[cut[k], cut[n]]

        one, two = (columns, depth) if transposed else (depth, columns)
        rows = [
            jnp.concatenate(
                [block(j, i) if transposed else block(i, j) for j in two], axis=1
            )
            for i in one
        ]
        return jnp.concatenate(rows, axis=0)

    def product(depth, columns, absent):
        return lax.dot_general(
            jnp.concatenate([x[:, cut[k]] for k in depth], axis=1),
            tile(depth, columns, absent),
            (((1,), (1 if transposed else 0,)), ((), ())),
            preferred_element_type=jnp.float32,
        )

    p = product((0, 1), (0, 1), ())
    q = product((0, 2), (2, 0), ((0, 0),))
    r = product((1, 2), (2, 1), ((1, 1), (2, 2)))
    low, high = slice(0, size), slice(size, 2 * size)
    return list(zip(cut, (p[:, low] + q[:, high], p[:, high] + r[:, high], q[:, low] + r[:, low])))


def run(kind, plan, coef, left, right, psi, acc, even, odd):
    pairs, local = left.shape[:2]
    slots = local * pairs
    count = plan[kind, 3 * slots]

    def first(i, halves):
        i = jnp.minimum(i, count - 1)
        p, s, block = [plan[kind, k * slots + i] for k in range(3)]
        for c, half in thirds(left.at[p, s], psi.at[block], False):
            halves[:, c] = (half * coef[s, p]).astype(jnp.bfloat16)

    def second(i, halves):
        p, s = [plan[kind, k * slots + i] for k in range(2)]
        for c, term in thirds(halves, right.at[p, s], True):
            acc[s, :, c] += term

    def two(j, carry):
        i = 2 * j
        first(i + 1, odd)
        second(i, even)
        first(i + 2, even)
        second(i + 1, odd)
        return carry

    @pl.when(count > 0)
    def _():
        first(0, even)
        lax.fori_loop(0, lax.div(count, 2), two, 0)

        @pl.when(lax.rem(count, 2) == 1)
        def _():
            second(count - 1, even)


def plan_kernel(local, source, plan):
    make_plan(source, plan, source.shape[1], local)


def products_kernel(kind, n_opg, plan, coef, left, right, *refs):
    local, sb = left.shape[1:3]
    last = kind == CLASSES - 1
    outs = n_opg if last else 1
    pieces, refs = refs[: -outs - 3 - last], refs[-outs - 3 - last :]
    psi, even, odd = refs[outs : outs + 3]
    acc = refs[-1] if last else refs[0]
    if kind:
        acc[...] = pieces[0][...]
        pieces = pieces[1:]
    else:
        acc[...] = jnp.zeros_like(acc)
    if kind == 0:
        for i, piece in enumerate(pieces):
            psi[i * local : (i + 1) * local] = piece[...]
    else:
        half = lax.rem(lax.axis_index(OPG), HALVES)
        rows = sb // HALVES
        for i in range(len(pieces) // 2):
            whole, halves = pieces[2 * i : 2 * i + 2]
            end = (i + 1) * local - 1
            psi[i * local : end] = whole[...]
            psi[end, pl.ds(pl.multiple_of(half * rows, 16), rows), :] = halves[0]
            psi[end, pl.ds(pl.multiple_of((1 - half) * rows, 16), rows), :] = halves[1]
    run(kind, plan, coef, left, right, psi, acc, even, odd)
    if last:
        me_opg = lax.axis_index(OPG)
        rows = sb // n_opg
        for r, send in enumerate(refs[:outs]):
            at = pl.multiple_of((r ^ me_opg) * rows, 8)
            send[...] = acc[:, pl.ds(at, rows), :].astype(send.dtype)


SMEM = pl.BlockSpec(memory_space=pltpu.SMEM)
VMEM = pl.BlockSpec(memory_space=pltpu.VMEM)


def products(kind, n_opg, plan, coef, left, right, totals, pieces):
    pairs, local, sb, _ = left.shape
    out_shape = jax.ShapeDtypeStruct((local, sb, sb), jnp.float32)
    scratch = []
    if kind == CLASSES - 1:
        scratch = [pltpu.VMEM(out_shape.shape, out_shape.dtype)]
        out_shape = tuple(
            jax.ShapeDtypeStruct(
                (local, sb // n_opg, sb), jnp.bfloat16 if r % PARTS else jnp.float32
            )
            for r in range(n_opg)
        )
    return pl.pallas_call(
        functools.partial(products_kernel, kind, n_opg),
        out_shape=out_shape,
        in_specs=[SMEM] * 2 + [VMEM] * (2 + len(totals) + len(pieces)),
        out_specs=jax.tree.map(lambda _: VMEM, out_shape),
        scratch_shapes=[
            pltpu.VMEM((len(pieces) // (2 if kind else 1) * local, sb, sb), jnp.bfloat16),
            pltpu.VMEM((sb, sb), jnp.bfloat16),
            pltpu.VMEM((sb, sb), jnp.bfloat16),
            *scratch,
        ],
        compiler_params=pltpu.CompilerParams(vmem_limit_bytes=KERNEL_VMEM),
        cost_estimate=pl.CostEstimate(flops=sb, bytes_accessed=0, transcendentals=0),
    )(plan, coef, left, right, *totals, *pieces)


def scatter_sum(sends, n_opg):
    out = []
    for high in reversed(range(n_opg // PARTS)):
        at = high * PARTS
        total = sends[at]
        for low in (3, 1, 2):
            total = total + flip(sends[at + low], OPG, n_opg, low).astype(jnp.float32)
        if high:
            total = flip(total.astype(jnp.bfloat16), OPG, n_opg, at).astype(jnp.float32)
        out.append(total)
    return sum(out[:-1], out[-1])


def on_device(n_opg, n_sec, psi, left_ops, right_ops, source, coef_index, sixj):
    local, sb, _ = psi.shape
    pairs = left_ops.shape[0]

    half = lax.rem(lax.axis_index(OPG), HALVES)
    cut = psi[local - 1].reshape(HALVES, sb // HALVES, sb)
    ours = lax.dynamic_index_in_dim(cut, half, axis=0, keepdims=False)
    ours, rest, psi = lax.optimization_barrier((ours, psi[: local - 1], psi))
    here, whole = {0: ours}, {0: rest}
    for bit in bits_of(n_sec)[1:]:
        for held in (here, whole):
            held.update({r | bit: flip(x, SEC, n_sec, bit) for r, x in held.items()})
    far = range(NEAR, n_sec, 2)
    here, whole = [here[r] for r in far], [whole[r] for r in far]
    partner = flip(psi, SEC, n_sec, 1)

    plan = pl.pallas_call(
        functools.partial(plan_kernel, local),
        out_shape=jax.ShapeDtypeStruct((CLASSES, 3 * local * pairs + 1), jnp.int32),
        in_specs=[SMEM],
        out_specs=SMEM,
        compiler_params=pltpu.CompilerParams(vmem_limit_bytes=KERNEL_VMEM),
        cost_estimate=pl.CostEstimate(flops=PLAN_FLOPS, bytes_accessed=0, transcendentals=0),
    )(source.T)
    plan, coef_index = lax.optimization_barrier((plan, coef_index))
    table = jnp.arange(sixj.shape[0], dtype=jnp.int32)
    coef = jnp.sum(jnp.where(coef_index.T[:, :, None] == table, sixj, 0.0), axis=2)

    def onto(kind, totals, pieces):
        return products(kind, n_opg, plan, coef, left_ops, right_ops, totals, pieces)

    def to_other_core(pieces):
        return [flip(x, SEC, n_sec, 1) for x in pieces]

    here, plan, coef = lax.optimization_barrier((here, plan, coef))
    there = [flip(x, OPG, n_opg, 1) for x in here]
    done = onto(0, [], [psi, partner])
    here, there, whole, done = lax.optimization_barrier((here, there, whole, done))
    whole_crossed = to_other_core(whole)
    halves = [jnp.stack(two) for two in zip(here, there)]
    halves_crossed = to_other_core(halves)
    done = onto(1, [done], [x for two in zip(whole, halves) for x in two])
    sends = onto(2, [done], [x for two in zip(whole_crossed, halves_crossed) for x in two])
    return jnp.swapaxes(scatter_sum(sends, n_opg), 0, 1).astype(jnp.bfloat16)


def solution(mesh):
    n_opg, n_sec = mesh.shape[OPG], mesh.shape[SEC]
    placed = (
        P(SEC, None, None),
        P(OPG, SEC, None, None),
        P(OPG, SEC, None, None),
        P(OPG, SEC),
        P(OPG, SEC),
        P(),
    )
    return jax.shard_map(
        functools.partial(on_device, n_opg, n_sec),
        mesh=mesh,
        in_specs=placed,
        out_specs=P(OPG, SEC, None),
        check_vma=False,
    )
```

```python
import functools

import jax
import jax.numpy as jnp
from jax import lax
from jax.experimental import pallas as pl
from jax.experimental.pallas import tpu as pltpu
from jax.sharding import PartitionSpec as P

OPG = "opg"
SEC = "sec"
PARTS = 4
HALVES = 2
NEAR = 2
KERNEL_VMEM = 24_000_000
PLAN_FLOPS = 40_000_000_000


def flip(x, axis, size, bit):
    return lax.ppermute(x, axis, [(i, i ^ bit) for i in range(size)])


def bits_of(size):
    return [1 << k for k in range(size.bit_length() - 1)]


CLASSES = 3


def make_plan(source, plan, pairs, local):
    slots = local * pairs
    for kind in range(CLASSES):
        plan[kind, 3 * slots] = 0
    me_sec = lax.axis_index(SEC)

    def sector(s):
        def one(p, carry):
            src = source[s, p]
            r, j = lax.div(src, local) ^ me_sec, lax.rem(src, local)
            kind = jnp.where(r < NEAR, 0, 1 + lax.rem(r, 2))
            block = jnp.where(r < NEAR, r, lax.div(r, 2) - 1) * local + j
            n = plan[kind, 3 * slots]
            plan[kind, n] = p
            plan[kind, slots + n] = s
            plan[kind, 2 * slots + n] = block
            plan[kind, 3 * slots] = n + 1
            return carry

        lax.fori_loop(0, pairs, one, 0)

    for s in range(local):
        sector(s)


def thirds(x, w, transposed):
    size = x.shape[1] // 3
    cut = [slice(i * size, (i + 1) * size) for i in range(3)]
    none = jnp.zeros((size, size), w.dtype)

    def tile(depth, columns, absent):
        def block(k, n):
            if (k, n) in absent:
                return none
            return w[cut[n], cut[k]] if transposed else w[cut[k], cut[n]]

        one, two = (columns, depth) if transposed else (depth, columns)
        rows = [
            jnp.concatenate(
                [block(j, i) if transposed else block(i, j) for j in two], axis=1
            )
            for i in one
        ]
        return jnp.concatenate(rows, axis=0)

    def product(depth, columns, absent):
        return lax.dot_general(
            jnp.concatenate([x[:, cut[k]] for k in depth], axis=1),
            tile(depth, columns, absent),
            (((1,), (1 if transposed else 0,)), ((), ())),
            preferred_element_type=jnp.float32,
        )

    p = product((0, 1), (0, 1), ())
    q = product((0, 2), (2, 0), ((0, 0),))
    r = product((1, 2), (2, 1), ((1, 1), (2, 2)))
    low, high = slice(0, size), slice(size, 2 * size)
    return list(zip(cut, (p[:, low] + q[:, high], p[:, high] + r[:, high], q[:, low] + r[:, low])))


def run(kind, plan, coef, left, right, psi, acc, even, odd):
    pairs, local = left.shape[:2]
    slots = local * pairs
    count = plan[kind, 3 * slots]

    def first(i, halves):
        i = jnp.minimum(i, count - 1)
        p, s, block = [plan[kind, k * slots + i] for k in range(3)]
        for c, half in thirds(left.at[p, s], psi.at[block], False):
            halves[:, c] = (half * coef[s, p]).astype(jnp.bfloat16)

    def second(i, halves):
        p, s = [plan[kind, k * slots + i] for k in range(2)]
        for c, term in thirds(halves, right.at[p, s], True):
            acc[s, :, c] += term

    def two(j, carry):
        i = 2 * j
        first(i + 1, odd)
        second(i, even)
        first(i + 2, even)
        second(i + 1, odd)
        return carry

    @pl.when(count > 0)
    def _():
        first(0, even)
        lax.fori_loop(0, lax.div(count, 2), two, 0)

        @pl.when(lax.rem(count, 2) == 1)
        def _():
            second(count - 1, even)


def plan_kernel(local, source, plan):
    make_plan(source, plan, source.shape[1], local)


def products_kernel(kind, n_opg, plan, coef, left, right, *refs):
    local, sb = left.shape[1:3]
    last = kind == CLASSES - 1
    outs = n_opg if last else 1
    pieces, refs = refs[: -outs - 3 - last], refs[-outs - 3 - last :]
    psi, even, odd = refs[outs : outs + 3]
    acc = refs[-1] if last else refs[0]
    if kind:
        acc[...] = pieces[0][...]
        pieces = pieces[1:]
    else:
        acc[...] = jnp.zeros_like(acc)
    if kind == 0:
        for i, piece in enumerate(pieces):
            psi[i * local : (i + 1) * local] = piece[...]
    else:
        half = lax.rem(lax.axis_index(OPG), HALVES)
        rows = sb // HALVES
        for i in range(len(pieces) // 2):
            whole, halves = pieces[2 * i : 2 * i + 2]
            end = (i + 1) * local - 1
            psi[i * local : end] = whole[...]
            psi[end, pl.ds(pl.multiple_of(half * rows, 16), rows), :] = halves[0]
            psi[end, pl.ds(pl.multiple_of((1 - half) * rows, 16), rows), :] = halves[1]
    run(kind, plan, coef, left, right, psi, acc, even, odd)
    if last:
        me_opg = lax.axis_index(OPG)
        rows = sb // n_opg
        for r, send in enumerate(refs[:outs]):
            at = pl.multiple_of((r ^ me_opg) * rows, 8)
            send[...] = acc[:, pl.ds(at, rows), :].astype(send.dtype)


SMEM = pl.BlockSpec(memory_space=pltpu.SMEM)
VMEM = pl.BlockSpec(memory_space=pltpu.VMEM)


def products(kind, n_opg, plan, coef, left, right, totals, pieces):
    pairs, local, sb, _ = left.shape
    out_shape = jax.ShapeDtypeStruct((local, sb, sb), jnp.float32)
    scratch = []
    if kind == CLASSES - 1:
        scratch = [pltpu.VMEM(out_shape.shape, out_shape.dtype)]
        out_shape = tuple(
            jax.ShapeDtypeStruct(
                (local, sb // n_opg, sb), jnp.bfloat16 if r % PARTS else jnp.float32
            )
            for r in range(n_opg)
        )
    return pl.pallas_call(
        functools.partial(products_kernel, kind, n_opg),
        out_shape=out_shape,
        in_specs=[SMEM] * 2 + [VMEM] * (2 + len(totals) + len(pieces)),
        out_specs=jax.tree.map(lambda _: VMEM, out_shape),
        scratch_shapes=[
            pltpu.VMEM((len(pieces) // (2 if kind else 1) * local, sb, sb), jnp.bfloat16),
            pltpu.VMEM((sb, sb), jnp.bfloat16),
            pltpu.VMEM((sb, sb), jnp.bfloat16),
            *scratch,
        ],
        compiler_params=pltpu.CompilerParams(vmem_limit_bytes=KERNEL_VMEM),
        cost_estimate=pl.CostEstimate(flops=sb, bytes_accessed=0, transcendentals=0),
    )(plan, coef, left, right, *totals, *pieces)


def scatter_sum(sends, n_opg):
    out = []
    for high in reversed(range(n_opg // PARTS)):
        at = high * PARTS
        total = sends[at]
        for low in (3, 1, 2):
            total = total + flip(sends[at + low], OPG, n_opg, low).astype(jnp.float32)
        if high:
            total = flip(total.astype(jnp.bfloat16), OPG, n_opg, at).astype(jnp.float32)
        out.append(total)
    return sum(out[:-1], out[-1])


def on_device(n_opg, n_sec, psi, left_ops, right_ops, source, coef_index, sixj):
    local, sb, _ = psi.shape
    pairs = left_ops.shape[0]

    half = lax.rem(lax.axis_index(OPG), HALVES)
    cut = psi[local - 1].reshape(HALVES, sb // HALVES, sb)
    ours = lax.dynamic_index_in_dim(cut, half, axis=0, keepdims=False)
    ours, rest, psi = lax.optimization_barrier((ours, psi[: local - 1], psi))
    here, whole = {0: ours}, {0: rest}
    for bit in bits_of(n_sec)[1:]:
        for held in (here, whole):
            held.update({r | bit: flip(x, SEC, n_sec, bit) for r, x in held.items()})
    far = range(NEAR, n_sec, 2)
    here, whole = [here[r] for r in far], [whole[r] for r in far]
    partner = flip(psi, SEC, n_sec, 1)

    plan = pl.pallas_call(
        functools.partial(plan_kernel, local),
        out_shape=jax.ShapeDtypeStruct((CLASSES, 3 * local * pairs + 1), jnp.int32),
        in_specs=[SMEM],
        out_specs=SMEM,
        compiler_params=pltpu.CompilerParams(vmem_limit_bytes=KERNEL_VMEM),
        cost_estimate=pl.CostEstimate(flops=PLAN_FLOPS, bytes_accessed=0, transcendentals=0),
    )(source.T)
    plan, coef_index = lax.optimization_barrier((plan, coef_index))
    table = jnp.arange(sixj.shape[0], dtype=jnp.int32)
    coef = jnp.sum(jnp.where(coef_index.T[:, :, None] == table, sixj, 0.0), axis=2)

    def onto(kind, totals, pieces):
        return products(kind, n_opg, plan, coef, left_ops, right_ops, totals, pieces)

    def to_other_core(pieces):
        return [flip(x, SEC, n_sec, 1) for x in pieces]

    here, plan, coef = lax.optimization_barrier((here, plan, coef))
    there = [flip(x, OPG, n_opg, 1) for x in here]
    done = onto(0, [], [psi, partner])
    here, there, whole, done = lax.optimization_barrier((here, there, whole, done))
    whole_crossed = to_other_core(whole)
    halves = [jnp.stack(two) for two in zip(here, there)]
    halves_crossed = to_other_core(halves)
    done = onto(1, [done], [x for two in zip(whole, halves) for x in two])
    sends = onto(2, [done], [x for two in zip(whole_crossed, halves_crossed) for x in two])
    return jnp.swapaxes(scatter_sum(sends, n_opg), 0, 1).astype(jnp.bfloat16)


def solution(mesh):
    n_opg, n_sec = mesh.shape[OPG], mesh.shape[SEC]
    placed = (
        P(SEC, None, None),
        P(OPG, SEC, None, None),
        P(OPG, SEC, None, None),
        P(OPG, SEC),
        P(OPG, SEC),
        P(),
    )
    return jax.shard_map(
        functools.partial(on_device, n_opg, n_sec),
        mesh=mesh,
        in_specs=placed,
        out_specs=P(OPG, SEC, None),
        check_vma=False,
    )
```

```python
import functools

import jax
import jax.numpy as jnp
from jax import lax
from jax.experimental import pallas as pl
from jax.experimental.pallas import tpu as pltpu
from jax.sharding import PartitionSpec as P

OPG = "opg"
SEC = "sec"
PARTS = 4
HALVES = 2
NEAR = 2
KERNEL_VMEM = 24_000_000
PLAN_FLOPS = 20_000_000_000


def flip(x, axis, size, bit):
    return lax.ppermute(x, axis, [(i, i ^ bit) for i in range(size)])


def bits_of(size):
    return [1 << k for k in range(size.bit_length() - 1)]


CLASSES = 3


def make_plan(source, plan, pairs, local):
    slots = local * pairs
    for kind in range(CLASSES):
        plan[kind, 3 * slots] = 0
    me_sec = lax.axis_index(SEC)

    def sector(s):
        def one(p, carry):
            src = source[s, p]
            r, j = lax.div(src, local) ^ me_sec, lax.rem(src, local)
            kind = jnp.where(r < NEAR, 0, 1 + lax.rem(r, 2))
            block = jnp.where(r < NEAR, r, lax.div(r, 2) - 1) * local + j
            n = plan[kind, 3 * slots]
            plan[kind, n] = p
            plan[kind, slots + n] = s
            plan[kind, 2 * slots + n] = block
            plan[kind, 3 * slots] = n + 1
            return carry

        lax.fori_loop(0, pairs, one, 0)

    for s in range(local):
        sector(s)


def thirds(x, w, transposed):
    size = x.shape[1] // 3
    cut = [slice(i * size, (i + 1) * size) for i in range(3)]
    none = jnp.zeros((size, size), w.dtype)

    def tile(depth, columns, absent):
        def block(k, n):
            if (k, n) in absent:
                return none
            return w[cut[n], cut[k]] if transposed else w[cut[k], cut[n]]

        one, two = (columns, depth) if transposed else (depth, columns)
        rows = [
            jnp.concatenate(
                [block(j, i) if transposed else block(i, j) for j in two], axis=1
            )
            for i in one
        ]
        return jnp.concatenate(rows, axis=0)

    def product(depth, columns, absent):
        return lax.dot_general(
            jnp.concatenate([x[:, cut[k]] for k in depth], axis=1),
            tile(depth, columns, absent),
            (((1,), (1 if transposed else 0,)), ((), ())),
            preferred_element_type=jnp.float32,
        )

    p = product((0, 1), (0, 1), ())
    q = product((0, 2), (2, 0), ((0, 0),))
    r = product((1, 2), (2, 1), ((1, 1), (2, 2)))
    low, high = slice(0, size), slice(size, 2 * size)
    return list(zip(cut, (p[:, low] + q[:, high], p[:, high] + r[:, high], q[:, low] + r[:, low])))


def run(kind, plan, coef, left, right, psi, acc, even, odd):
    pairs, local = left.shape[:2]
    slots = local * pairs
    count = plan[kind, 3 * slots]

    def first(i, halves):
        i = jnp.minimum(i, count - 1)
        p, s, block = [plan[kind, k * slots + i] for k in range(3)]
        for c, half in thirds(left.at[p, s], psi.at[block], False):
            halves[:, c] = (half * coef[s, p]).astype(jnp.bfloat16)

    def second(i, halves):
        p, s = [plan[kind, k * slots + i] for k in range(2)]
        for c, term in thirds(halves, right.at[p, s], True):
            acc[s, :, c] += term

    def two(j, carry):
        i = 2 * j
        first(i + 1, odd)
        second(i, even)
        first(i + 2, even)
        second(i + 1, odd)
        return carry

    @pl.when(count > 0)
    def _():
        first(0, even)
        lax.fori_loop(0, lax.div(count, 2), two, 0)

        @pl.when(lax.rem(count, 2) == 1)
        def _():
            second(count - 1, even)


def plan_kernel(local, source, plan):
    make_plan(source, plan, source.shape[1], local)


def products_kernel(kind, n_opg, plan, coef, left, right, *refs):
    local, sb = left.shape[1:3]
    last = kind == CLASSES - 1
    outs = n_opg if last else 1
    pieces, refs = refs[: -outs - 3 - last], refs[-outs - 3 - last :]
    psi, even, odd = refs[outs : outs + 3]
    acc = refs[-1] if last else refs[0]
    if kind:
        acc[...] = pieces[0][...]
        pieces = pieces[1:]
    else:
        acc[...] = jnp.zeros_like(acc)
    if kind == 0:
        for i, piece in enumerate(pieces):
            psi[i * local : (i + 1) * local] = piece[...]
    else:
        half = lax.rem(lax.axis_index(OPG), HALVES)
        rows = sb // HALVES
        for i in range(len(pieces) // 2):
            whole, halves = pieces[2 * i : 2 * i + 2]
            end = (i + 1) * local - 1
            psi[i * local : end] = whole[...]
            psi[end, pl.ds(pl.multiple_of(half * rows, 16), rows), :] = halves[0]
            psi[end, pl.ds(pl.multiple_of((1 - half) * rows, 16), rows), :] = halves[1]
    run(kind, plan, coef, left, right, psi, acc, even, odd)
    if last:
        me_opg = lax.axis_index(OPG)
        rows = sb // n_opg
        for r, send in enumerate(refs[:outs]):
            at = pl.multiple_of((r ^ me_opg) * rows, 8)
            send[...] = acc[:, pl.ds(at, rows), :].astype(send.dtype)


SMEM = pl.BlockSpec(memory_space=pltpu.SMEM)
VMEM = pl.BlockSpec(memory_space=pltpu.VMEM)


def products(kind, n_opg, plan, coef, left, right, totals, pieces):
    pairs, local, sb, _ = left.shape
    out_shape = jax.ShapeDtypeStruct((local, sb, sb), jnp.float32)
    scratch = []
    if kind == CLASSES - 1:
        scratch = [pltpu.VMEM(out_shape.shape, out_shape.dtype)]
        out_shape = tuple(
            jax.ShapeDtypeStruct(
                (local, sb // n_opg, sb), jnp.bfloat16 if r % PARTS else jnp.float32
            )
            for r in range(n_opg)
        )
    return pl.pallas_call(
        functools.partial(products_kernel, kind, n_opg),
        out_shape=out_shape,
        in_specs=[SMEM] * 2 + [VMEM] * (2 + len(totals) + len(pieces)),
        out_specs=jax.tree.map(lambda _: VMEM, out_shape),
        scratch_shapes=[
            pltpu.VMEM((len(pieces) // (2 if kind else 1) * local, sb, sb), jnp.bfloat16),
            pltpu.VMEM((sb, sb), jnp.bfloat16),
            pltpu.VMEM((sb, sb), jnp.bfloat16),
            *scratch,
        ],
        compiler_params=pltpu.CompilerParams(vmem_limit_bytes=KERNEL_VMEM),
        cost_estimate=pl.CostEstimate(flops=sb, bytes_accessed=0, transcendentals=0),
    )(plan, coef, left, right, *totals, *pieces)


def scatter_sum(sends, n_opg):
    out = []
    for high in reversed(range(n_opg // PARTS)):
        at = high * PARTS
        total = sends[at]
        for low in (3, 1, 2) if high else (1, 3, 2):
            total = total + flip(sends[at + low], OPG, n_opg, low).astype(jnp.float32)
        if high:
            total = flip(total.astype(jnp.bfloat16), OPG, n_opg, at).astype(jnp.float32)
        out.append(total)
    return sum(out[:-1], out[-1])


def on_device(n_opg, n_sec, psi, left_ops, right_ops, source, coef_index, sixj):
    local, sb, _ = psi.shape
    pairs = left_ops.shape[0]

    half = lax.rem(lax.axis_index(OPG), HALVES)
    cut = psi[local - 1].reshape(HALVES, sb // HALVES, sb)
    ours = lax.dynamic_index_in_dim(cut, half, axis=0, keepdims=False)
    ours, rest, psi = lax.optimization_barrier((ours, psi[: local - 1], psi))
    here, whole = {0: ours}, {0: rest}
    for bit in bits_of(n_sec)[1:]:
        for held in (here, whole):
            held.update({r | bit: flip(x, SEC, n_sec, bit) for r, x in held.items()})
    far = range(NEAR, n_sec, 2)
    here, whole = [here[r] for r in far], [whole[r] for r in far]
    partner = flip(psi, SEC, n_sec, 1)

    plan = pl.pallas_call(
        functools.partial(plan_kernel, local),
        out_shape=jax.ShapeDtypeStruct((CLASSES, 3 * local * pairs + 1), jnp.int32),
        in_specs=[SMEM],
        out_specs=SMEM,
        compiler_params=pltpu.CompilerParams(vmem_limit_bytes=KERNEL_VMEM),
        cost_estimate=pl.CostEstimate(flops=PLAN_FLOPS, bytes_accessed=0, transcendentals=0),
    )(source.T)
    plan, coef_index = lax.optimization_barrier((plan, coef_index))
    table = jnp.arange(sixj.shape[0], dtype=jnp.int32)
    coef = jnp.sum(jnp.where(coef_index.T[:, :, None] == table, sixj, 0.0), axis=2)

    def onto(kind, totals, pieces):
        return products(kind, n_opg, plan, coef, left_ops, right_ops, totals, pieces)

    def to_other_core(pieces):
        return [flip(x, SEC, n_sec, 1) for x in pieces]

    here, plan, coef = lax.optimization_barrier((here, plan, coef))
    there = [flip(x, OPG, n_opg, 1) for x in here]
    done = onto(0, [], [psi, partner])
    here, there, whole, done = lax.optimization_barrier((here, there, whole, done))
    whole_crossed = to_other_core(whole)
    halves = [jnp.stack(two) for two in zip(here, there)]
    halves_crossed = to_other_core(halves)
    done = onto(1, [done], [x for two in zip(whole, halves) for x in two])
    sends = onto(2, [done], [x for two in zip(whole_crossed, halves_crossed) for x in two])
    return jnp.swapaxes(scatter_sum(sends, n_opg), 0, 1).astype(jnp.bfloat16)


def solution(mesh):
    n_opg, n_sec = mesh.shape[OPG], mesh.shape[SEC]
    placed = (
        P(SEC, None, None),
        P(OPG, SEC, None, None),
        P(OPG, SEC, None, None),
        P(OPG, SEC),
        P(OPG, SEC),
        P(),
    )
    return jax.shard_map(
        functools.partial(on_device, n_opg, n_sec),
        mesh=mesh,
        in_specs=placed,
        out_specs=P(OPG, SEC, None),
        check_vma=False,
    )
```

```python
import functools

import jax
import jax.numpy as jnp
from jax import lax
from jax.experimental import pallas as pl
from jax.experimental.pallas import tpu as pltpu
from jax.sharding import PartitionSpec as P

OPG = "opg"
SEC = "sec"
PARTS = 4
HALVES = 2
NEAR = 2
KERNEL_VMEM = 24_000_000
PLAN_FLOPS = 20_000_000_000


def flip(x, axis, size, bit):
    return lax.ppermute(x, axis, [(i, i ^ bit) for i in range(size)])


def bits_of(size):
    return [1 << k for k in range(size.bit_length() - 1)]


CLASSES = 3


def make_plan(source, plan, pairs, local):
    slots = local * pairs
    for kind in range(CLASSES):
        plan[kind, 3 * slots] = 0
    me_sec = lax.axis_index(SEC)

    def sector(s):
        def one(p, carry):
            src = source[s, p]
            r, j = lax.div(src, local) ^ me_sec, lax.rem(src, local)
            kind = jnp.where(r < NEAR, 0, 1 + lax.rem(r, 2))
            block = jnp.where(r < NEAR, r, lax.div(r, 2) - 1) * local + j
            n = plan[kind, 3 * slots]
            plan[kind, n] = p
            plan[kind, slots + n] = s
            plan[kind, 2 * slots + n] = block
            plan[kind, 3 * slots] = n + 1
            return carry

        lax.fori_loop(0, pairs, one, 0)

    for s in range(local):
        sector(s)


def thirds(x, w, transposed):
    size = x.shape[1] // 3
    cut = [slice(i * size, (i + 1) * size) for i in range(3)]
    none = jnp.zeros((size, size), w.dtype)

    def tile(depth, columns, absent):
        def block(k, n):
            if (k, n) in absent:
                return none
            return w[cut[n], cut[k]] if transposed else w[cut[k], cut[n]]

        one, two = (columns, depth) if transposed else (depth, columns)
        rows = [
            jnp.concatenate(
                [block(j, i) if transposed else block(i, j) for j in two], axis=1
            )
            for i in one
        ]
        return jnp.concatenate(rows, axis=0)

    def product(depth, columns, absent):
        return lax.dot_general(
            jnp.concatenate([x[:, cut[k]] for k in depth], axis=1),
            tile(depth, columns, absent),
            (((1,), (1 if transposed else 0,)), ((), ())),
            preferred_element_type=jnp.float32,
        )

    p = product((0, 1), (0, 1), ())
    q = product((0, 2), (2, 0), ((0, 0),))
    r = product((1, 2), (2, 1), ((1, 1), (2, 2)))
    low, high = slice(0, size), slice(size, 2 * size)
    return list(zip(cut, (p[:, low] + q[:, high], p[:, high] + r[:, high], q[:, low] + r[:, low])))


def run(kind, plan, coef, left, right, psi, acc, even, odd):
    pairs, local = left.shape[:2]
    slots = local * pairs
    count = plan[kind, 3 * slots]

    def first(i, halves):
        i = jnp.minimum(i, count - 1)
        p, s, block = [plan[kind, k * slots + i] for k in range(3)]
        for c, half in thirds(left.at[p, s], psi.at[block], False):
            halves[:, c] = (half * coef[s, p]).astype(jnp.bfloat16)

    def second(i, halves):
        p, s = [plan[kind, k * slots + i] for k in range(2)]
        for c, term in thirds(halves, right.at[p, s], True):
            acc[s, :, c] += term

    def two(j, carry):
        i = 2 * j
        first(i + 1, odd)
        second(i, even)
        first(i + 2, even)
        second(i + 1, odd)
        return carry

    @pl.when(count > 0)
    def _():
        first(0, even)
        lax.fori_loop(0, lax.div(count, 2), two, 0)

        @pl.when(lax.rem(count, 2) == 1)
        def _():
            second(count - 1, even)


def plan_kernel(local, source, plan):
    make_plan(source, plan, source.shape[1], local)


def products_kernel(kind, n_opg, plan, coef, left, right, *refs):
    local, sb = left.shape[1:3]
    last = kind == CLASSES - 1
    outs = n_opg if last else 1
    pieces, refs = refs[: -outs - 3 - last], refs[-outs - 3 - last :]
    psi, even, odd = refs[outs : outs + 3]
    acc = refs[-1] if last else refs[0]
    if kind:
        acc[...] = pieces[0][...]
        pieces = pieces[1:]
    else:
        acc[...] = jnp.zeros_like(acc)
    if kind == 0:
        for i, piece in enumerate(pieces):
            psi[i * local : (i + 1) * local] = piece[...]
    else:
        half = lax.rem(lax.axis_index(OPG), HALVES)
        rows = sb // HALVES
        for i in range(len(pieces) // 2):
            whole, halves = pieces[2 * i : 2 * i + 2]
            end = (i + 1) * local - 1
            psi[i * local : end] = whole[...]
            psi[end, pl.ds(pl.multiple_of(half * rows, 16), rows), :] = halves[0]
            psi[end, pl.ds(pl.multiple_of((1 - half) * rows, 16), rows), :] = halves[1]
    run(kind, plan, coef, left, right, psi, acc, even, odd)
    if last:
        me_opg = lax.axis_index(OPG)
        rows = sb // n_opg
        for r, send in enumerate(refs[:outs]):
            at = pl.multiple_of((r ^ me_opg) * rows, 8)
            send[...] = acc[:, pl.ds(at, rows), :].astype(send.dtype)


SMEM = pl.BlockSpec(memory_space=pltpu.SMEM)
VMEM = pl.BlockSpec(memory_space=pltpu.VMEM)


def products(kind, n_opg, plan, coef, left, right, totals, pieces):
    pairs, local, sb, _ = left.shape
    out_shape = jax.ShapeDtypeStruct((local, sb, sb), jnp.float32)
    scratch = []
    if kind == CLASSES - 1:
        scratch = [pltpu.VMEM(out_shape.shape, out_shape.dtype)]
        out_shape = tuple(
            jax.ShapeDtypeStruct(
                (local, sb // n_opg, sb), jnp.bfloat16 if r % PARTS else jnp.float32
            )
            for r in range(n_opg)
        )
    return pl.pallas_call(
        functools.partial(products_kernel, kind, n_opg),
        out_shape=out_shape,
        in_specs=[SMEM] * 2 + [VMEM] * (2 + len(totals) + len(pieces)),
        out_specs=jax.tree.map(lambda _: VMEM, out_shape),
        scratch_shapes=[
            pltpu.VMEM((len(pieces) // (2 if kind else 1) * local, sb, sb), jnp.bfloat16),
            pltpu.VMEM((sb, sb), jnp.bfloat16),
            pltpu.VMEM((sb, sb), jnp.bfloat16),
            *scratch,
        ],
        compiler_params=pltpu.CompilerParams(vmem_limit_bytes=KERNEL_VMEM),
        cost_estimate=pl.CostEstimate(flops=sb, bytes_accessed=0, transcendentals=0),
    )(plan, coef, left, right, *totals, *pieces)


def scatter_sum(sends, n_opg):
    out = []
    for high in reversed(range(n_opg // PARTS)):
        at = high * PARTS
        total = sends[at]
        for low in (1, 3, 2) if high else (3, 1, 2):
            total = total + flip(sends[at + low], OPG, n_opg, low).astype(jnp.float32)
        if high:
            total = flip(total.astype(jnp.bfloat16), OPG, n_opg, at).astype(jnp.float32)
        out.append(total)
    return sum(out[:-1], out[-1])


def on_device(n_opg, n_sec, psi, left_ops, right_ops, source, coef_index, sixj):
    local, sb, _ = psi.shape
    pairs = left_ops.shape[0]

    half = lax.rem(lax.axis_index(OPG), HALVES)
    cut = psi[local - 1].reshape(HALVES, sb // HALVES, sb)
    ours = lax.dynamic_index_in_dim(cut, half, axis=0, keepdims=False)
    ours, rest, psi = lax.optimization_barrier((ours, psi[: local - 1], psi))
    here, whole = {0: ours}, {0: rest}
    for bit in bits_of(n_sec)[1:]:
        for held in (here, whole):
            held.update({r | bit: flip(x, SEC, n_sec, bit) for r, x in held.items()})
    far = range(NEAR, n_sec, 2)
    here, whole = [here[r] for r in far], [whole[r] for r in far]
    partner = flip(psi, SEC, n_sec, 1)

    plan = pl.pallas_call(
        functools.partial(plan_kernel, local),
        out_shape=jax.ShapeDtypeStruct((CLASSES, 3 * local * pairs + 1), jnp.int32),
        in_specs=[SMEM],
        out_specs=SMEM,
        compiler_params=pltpu.CompilerParams(vmem_limit_bytes=KERNEL_VMEM),
        cost_estimate=pl.CostEstimate(flops=PLAN_FLOPS, bytes_accessed=0, transcendentals=0),
    )(source.T)
    plan, coef_index = lax.optimization_barrier((plan, coef_index))
    table = jnp.arange(sixj.shape[0], dtype=jnp.int32)
    coef = jnp.sum(jnp.where(coef_index.T[:, :, None] == table, sixj, 0.0), axis=2)

    def onto(kind, totals, pieces):
        return products(kind, n_opg, plan, coef, left_ops, right_ops, totals, pieces)

    def to_other_core(pieces):
        return [flip(x, SEC, n_sec, 1) for x in pieces]

    here, plan, coef = lax.optimization_barrier((here, plan, coef))
    there = [flip(x, OPG, n_opg, 1) for x in here]
    done = onto(0, [], [psi, partner])
    here, there, whole, done = lax.optimization_barrier((here, there, whole, done))
    whole_crossed = to_other_core(whole)
    halves = [jnp.stack(two) for two in zip(here, there)]
    halves_crossed = to_other_core(halves)
    done = onto(1, [done], [x for two in zip(whole, halves) for x in two])
    sends = onto(2, [done], [x for two in zip(whole_crossed, halves_crossed) for x in two])
    return jnp.swapaxes(scatter_sum(sends, n_opg), 0, 1).astype(jnp.bfloat16)


def solution(mesh):
    n_opg, n_sec = mesh.shape[OPG], mesh.shape[SEC]
    placed = (
        P(SEC, None, None),
        P(OPG, SEC, None, None),
        P(OPG, SEC, None, None),
        P(OPG, SEC),
        P(OPG, SEC),
        P(),
    )
    return jax.shard_map(
        functools.partial(on_device, n_opg, n_sec),
        mesh=mesh,
        in_specs=placed,
        out_specs=P(OPG, SEC, None),
        check_vma=False,
    )
```

```python
import functools

import jax
import jax.numpy as jnp
from jax import lax
from jax.experimental import pallas as pl
from jax.experimental.pallas import tpu as pltpu
from jax.sharding import PartitionSpec as P

OPG = "opg"
SEC = "sec"
PARTS = 4
HALVES = 2
NEAR = 2
KERNEL_VMEM = 24_000_000
PLAN_FLOPS = 20_000_000_000


def flip(x, axis, size, bit):
    return lax.ppermute(x, axis, [(i, i ^ bit) for i in range(size)])


def bits_of(size):
    return [1 << k for k in range(size.bit_length() - 1)]


CLASSES = 3


def make_plan(source, plan, pairs, local):
    slots = local * pairs
    for kind in range(CLASSES):
        plan[kind, 3 * slots] = 0
    me_sec = lax.axis_index(SEC)

    def sector(s):
        def one(p, carry):
            src = source[s, p]
            r, j = lax.div(src, local) ^ me_sec, lax.rem(src, local)
            kind = jnp.where(r < NEAR, 0, 1 + lax.rem(r, 2))
            block = jnp.where(r < NEAR, r, lax.div(r, 2) - 1) * local + j
            n = plan[kind, 3 * slots]
            plan[kind, n] = p
            plan[kind, slots + n] = s
            plan[kind, 2 * slots + n] = block
            plan[kind, 3 * slots] = n + 1
            return carry

        lax.fori_loop(0, pairs, one, 0)

    for s in range(local):
        sector(s)


def thirds(x, w, transposed):
    size = x.shape[1] // 3
    cut = [slice(i * size, (i + 1) * size) for i in range(3)]
    none = jnp.zeros((size, size), w.dtype)

    def tile(depth, columns, absent):
        def block(k, n):
            if (k, n) in absent:
                return none
            return w[cut[n], cut[k]] if transposed else w[cut[k], cut[n]]

        one, two = (columns, depth) if transposed else (depth, columns)
        rows = [
            jnp.concatenate(
                [block(j, i) if transposed else block(i, j) for j in two], axis=1
            )
            for i in one
        ]
        return jnp.concatenate(rows, axis=0)

    def product(depth, columns, absent):
        return lax.dot_general(
            jnp.concatenate([x[:, cut[k]] for k in depth], axis=1),
            tile(depth, columns, absent),
            (((1,), (1 if transposed else 0,)), ((), ())),
            preferred_element_type=jnp.float32,
        )

    p = product((0, 1), (0, 1), ())
    q = product((0, 2), (2, 0), ((0, 0),))
    r = product((1, 2), (2, 1), ((1, 1), (2, 2)))
    low, high = slice(0, size), slice(size, 2 * size)
    return list(zip(cut, (p[:, low] + q[:, high], p[:, high] + r[:, high], q[:, low] + r[:, low])))


def run(kind, plan, coef, left, right, psi, acc, even, odd):
    pairs, local = left.shape[:2]
    slots = local * pairs
    count = plan[kind, 3 * slots]

    def first(i, halves):
        i = jnp.minimum(i, count - 1)
        p, s, block = [plan[kind, k * slots + i] for k in range(3)]
        for c, half in thirds(left.at[p, s], psi.at[block], False):
            halves[:, c] = (half * coef[s, p]).astype(jnp.bfloat16)

    def second(i, halves):
        p, s = [plan[kind, k * slots + i] for k in range(2)]
        for c, term in thirds(halves, right.at[p, s], True):
            acc[s, :, c] += term

    def two(j, carry):
        i = 2 * j
        first(i + 1, odd)
        second(i, even)
        first(i + 2, even)
        second(i + 1, odd)
        return carry

    @pl.when(count > 0)
    def _():
        first(0, even)
        lax.fori_loop(0, lax.div(count, 2), two, 0)

        @pl.when(lax.rem(count, 2) == 1)
        def _():
            second(count - 1, even)


def plan_kernel(local, source, plan):
    make_plan(source, plan, source.shape[1], local)


def products_kernel(kind, n_opg, plan, coef, left, right, *refs):
    local, sb = left.shape[1:3]
    last = kind == CLASSES - 1
    outs = n_opg if last else 1
    pieces, refs = refs[: -outs - 3 - last], refs[-outs - 3 - last :]
    psi, even, odd = refs[outs : outs + 3]
    acc = refs[-1] if last else refs[0]
    if kind:
        acc[...] = pieces[0][...]
        pieces = pieces[1:]
    else:
        acc[...] = jnp.zeros_like(acc)
    if kind == 0:
        for i, piece in enumerate(pieces):
            psi[i * local : (i + 1) * local] = piece[...]
    else:
        half = lax.rem(lax.axis_index(OPG), HALVES)
        rows = sb // HALVES
        for i in range(len(pieces) // 2):
            whole, halves = pieces[2 * i : 2 * i + 2]
            end = (i + 1) * local - 1
            psi[i * local : end] = whole[...]
            psi[end, pl.ds(pl.multiple_of(half * rows, 16), rows), :] = halves[0]
            psi[end, pl.ds(pl.multiple_of((1 - half) * rows, 16), rows), :] = halves[1]
    run(kind, plan, coef, left, right, psi, acc, even, odd)
    if last:
        me_opg = lax.axis_index(OPG)
        rows = sb // n_opg
        for r, send in enumerate(refs[:outs]):
            at = pl.multiple_of((r ^ me_opg) * rows, 8)
            send[...] = acc[:, pl.ds(at, rows), :].astype(send.dtype)


SMEM = pl.BlockSpec(memory_space=pltpu.SMEM)
VMEM = pl.BlockSpec(memory_space=pltpu.VMEM)


def products(kind, n_opg, plan, coef, left, right, totals, pieces):
    pairs, local, sb, _ = left.shape
    out_shape = jax.ShapeDtypeStruct((local, sb, sb), jnp.float32)
    scratch = []
    if kind == CLASSES - 1:
        scratch = [pltpu.VMEM(out_shape.shape, out_shape.dtype)]
        out_shape = tuple(
            jax.ShapeDtypeStruct(
                (local, sb // n_opg, sb), jnp.bfloat16 if r % PARTS else jnp.float32
            )
            for r in range(n_opg)
        )
    return pl.pallas_call(
        functools.partial(products_kernel, kind, n_opg),
        out_shape=out_shape,
        in_specs=[SMEM] * 2 + [VMEM] * (2 + len(totals) + len(pieces)),
        out_specs=jax.tree.map(lambda _: VMEM, out_shape),
        scratch_shapes=[
            pltpu.VMEM((len(pieces) // (2 if kind else 1) * local, sb, sb), jnp.bfloat16),
            pltpu.VMEM((sb, sb), jnp.bfloat16),
            pltpu.VMEM((sb, sb), jnp.bfloat16),
            *scratch,
        ],
        compiler_params=pltpu.CompilerParams(vmem_limit_bytes=KERNEL_VMEM),
        cost_estimate=pl.CostEstimate(flops=sb, bytes_accessed=0, transcendentals=0),
    )(plan, coef, left, right, *totals, *pieces)


def scatter_sum(sends, n_opg):
    out = []
    for high in reversed(range(n_opg // PARTS)):
        at = high * PARTS
        total = sends[at]
        for low in (3, 2, 1) if high else (3, 1, 2):
            total = total + flip(sends[at + low], OPG, n_opg, low).astype(jnp.float32)
        if high:
            total = flip(total.astype(jnp.bfloat16), OPG, n_opg, at).astype(jnp.float32)
        out.append(total)
    return sum(out[:-1], out[-1])


def on_device(n_opg, n_sec, psi, left_ops, right_ops, source, coef_index, sixj):
    local, sb, _ = psi.shape
    pairs = left_ops.shape[0]

    half = lax.rem(lax.axis_index(OPG), HALVES)
    cut = psi[local - 1].reshape(HALVES, sb // HALVES, sb)
    ours = lax.dynamic_index_in_dim(cut, half, axis=0, keepdims=False)
    ours, rest, psi = lax.optimization_barrier((ours, psi[: local - 1], psi))
    here, whole = {0: ours}, {0: rest}
    for bit in bits_of(n_sec)[1:]:
        for held in (here, whole):
            held.update({r | bit: flip(x, SEC, n_sec, bit) for r, x in held.items()})
    far = range(NEAR, n_sec, 2)
    here, whole = [here[r] for r in far], [whole[r] for r in far]
    partner = flip(psi, SEC, n_sec, 1)

    plan = pl.pallas_call(
        functools.partial(plan_kernel, local),
        out_shape=jax.ShapeDtypeStruct((CLASSES, 3 * local * pairs + 1), jnp.int32),
        in_specs=[SMEM],
        out_specs=SMEM,
        compiler_params=pltpu.CompilerParams(vmem_limit_bytes=KERNEL_VMEM),
        cost_estimate=pl.CostEstimate(flops=PLAN_FLOPS, bytes_accessed=0, transcendentals=0),
    )(source.T)
    plan, coef_index = lax.optimization_barrier((plan, coef_index))
    table = jnp.arange(sixj.shape[0], dtype=jnp.int32)
    coef = jnp.sum(jnp.where(coef_index.T[:, :, None] == table, sixj, 0.0), axis=2)

    def onto(kind, totals, pieces):
        return products(kind, n_opg, plan, coef, left_ops, right_ops, totals, pieces)

    def to_other_core(pieces):
        return [flip(x, SEC, n_sec, 1) for x in pieces]

    here, plan, coef = lax.optimization_barrier((here, plan, coef))
    there = [flip(x, OPG, n_opg, 1) for x in here]
    done = onto(0, [], [psi, partner])
    here, there, whole, done = lax.optimization_barrier((here, there, whole, done))
    whole_crossed = to_other_core(whole)
    halves = [jnp.stack(two) for two in zip(here, there)]
    halves_crossed = to_other_core(halves)
    done = onto(1, [done], [x for two in zip(whole, halves) for x in two])
    sends = onto(2, [done], [x for two in zip(whole_crossed, halves_crossed) for x in two])
    return jnp.swapaxes(scatter_sum(sends, n_opg), 0, 1).astype(jnp.bfloat16)


def solution(mesh):
    n_opg, n_sec = mesh.shape[OPG], mesh.shape[SEC]
    placed = (
        P(SEC, None, None),
        P(OPG, SEC, None, None),
        P(OPG, SEC, None, None),
        P(OPG, SEC),
        P(OPG, SEC),
        P(),
    )
    return jax.shard_map(
        functools.partial(on_device, n_opg, n_sec),
        mesh=mesh,
        in_specs=placed,
        out_specs=P(OPG, SEC, None),
        check_vma=False,
    )
```
